256 devices in a mesh: row: 16 (over y_lo, x, core), col: 16 (over y_hi, z).
Axes of the slice: x: 4, y: 4 (y_hi: 2, y_lo: 2; y = y_hi * 2 + y_lo), z: 8, core: 2. Of those that a mesh axis runs over, the one named last changes fastest.
Arguments:
- pair: float32 [384, 384, 128], P('row', 'col'), may hold values from -6 to 6
- grad_out: float32 [384, 384, 128], P('row', 'col'), may hold values from -6 to 6
- w_in_out: bfloat16 [128, 384], replicated, may hold values from -0.5 to 0.5
- w_out_out: bfloat16 [64, 128], replicated, may hold values from -0.75 to 0.75
- w_in_in: bfloat16 [128, 384], replicated, may hold values from -0.5 to 0.5
- w_out_in: bfloat16 [64, 128], replicated, may hold values from -0.75 to 0.75
Outputs:
- pair_new: float32 [384, 384, 128], P('row', 'col')
- pair_grad: float32 [384, 384, 128], P('row', 'col')
- grad_win_out: float32 [128, 384], replicated
- grad_wout_out: float32 [64, 128], replicated
- grad_win_in: float32 [128, 384], replicated
- grad_wout_in: float32 [64, 128], replicated
The draws below stay inside these ranges and needn't reach their ends.
All inputs are finite; a program needn't handle non-finite values.
Results may differ from the reference program's by a relative error of at most 0.035.
Values may be sent and summed in bfloat16 or wider, within the bound.
No kernel may reach another device: no remote copies, remote signals or barrier semaphores. Data moves between devices by JAX's collectives and lax.ppermute only.
A program may use at most 64 MiB of HBM per device.

```python
import jax
import jax.numpy as jnp
from jax import lax

C = 128
HID = 64
N = 384


def block_scale(stream_key, extent, split, low, high):
    factor_of = 1.0
    for dim, parts in split:
        draws = jax.random.uniform(jax.random.fold_in(jax.random.fold_in(stream_key, 6), dim), (parts,), jnp.float32, low / len(split), high / len(split))
        factor_of = factor_of * jnp.repeat(jnp.exp(draws), extent[dim] // parts).reshape((-1,) + (1,) * (len(extent) - 1 - dim))
    return factor_of


def normal_values(own_key, dims, scale, bound, cuts=(), dtype=jnp.bfloat16):
    entries = scale * jax.random.normal(own_key, dims, jnp.float32)
    if cuts:
        entries = entries * block_scale(own_key, dims, cuts, -0.22, 0.18)
    return jnp.clip(entries, -bound, bound).astype(dtype)


def setup_inputs(seed: int = 0) -> dict:
    keys = jax.random.split(jax.random.key(seed), 7)
    return {
        "pair": normal_values(keys[0], (N, N, C), 1.0, 6.0, ((0, 16), (1, 16)), jnp.float32),
        "grad_out": normal_values(keys[1], (N, N, C), 1.0, 6.0, ((0, 16), (1, 16)), jnp.float32),
        "w_in_out": normal_values(keys[2], (C, 4 * HID + C), C ** -0.5, 0.5),
        "w_out_out": normal_values(keys[3], (HID, C), HID ** -0.5, 0.75),
        "w_in_in": normal_values(keys[4], (C, 4 * HID + C), C ** -0.5, 0.5),
        "w_out_in": normal_values(keys[5], (HID, C), HID ** -0.5, 0.75),
    }


EPS = 1e-05
HIGH = lax.Precision.HIGHEST

def layer_norm(values):
    center = values - lax.optimization_barrier(jnp.mean(values, axis=-1, keepdims=True))
    spread = lax.optimization_barrier(jnp.mean(center * center, axis=-1, keepdims=True))
    return center * lax.rsqrt(spread + EPS)

def gating(projected):
    left = (jax.nn.sigmoid(projected[..., HID:2 * HID]) * projected[..., :HID]).astype(jnp.bfloat16)
    right = (jax.nn.sigmoid(projected[..., 3 * HID:4 * HID]) * projected[..., 2 * HID:3 * HID]).astype(jnp.bfloat16)
    gate = jax.nn.sigmoid(projected[..., 4 * HID:])
    return (left, right, gate)

def prepare(pair, w_in):
    normed = layer_norm(pair).astype(jnp.bfloat16)
    projected = jnp.dot(normed, w_in, preferred_element_type=jnp.float32)
    return (normed, projected)

def finish(mixed, pair, gate, w_out):
    post = layer_norm(mixed).astype(jnp.bfloat16)
    return pair + gate * jnp.dot(post, w_out, preferred_element_type=jnp.float32)

def finish_back(grad_new, mixed, gate, w_out):
    post = layer_norm(mixed).astype(jnp.bfloat16)
    projected_out = jnp.dot(post, w_out, preferred_element_type=jnp.float32)
    grad_gate = grad_new * projected_out
    grad_proj = grad_new * gate
    grad_w = jnp.dot(post.reshape(-1, HID).astype(jnp.float32).T, grad_proj.reshape(-1, C), precision=HIGH)
    grad_post = jnp.dot(grad_proj, w_out.astype(jnp.float32).T, precision=HIGH)
    _, pull = jax.vjp(layer_norm, mixed)
    return (pull(grad_post)[0], grad_gate, grad_w)

def prepare_back(pair, normed, projected, grad_left, grad_right, grad_gate, w_in):
    _, pull = jax.vjp(gating, projected)
    grad_projected = pull((grad_left, grad_right, grad_gate))[0]
    width = grad_projected.shape[-1]
    grad_w = jnp.dot(normed.reshape(-1, C).astype(jnp.float32).T, grad_projected.reshape(-1, width), precision=HIGH)
    grad_normed = jnp.dot(grad_projected, w_in.astype(jnp.float32).T, precision=HIGH)
    _, pull_norm = jax.vjp(layer_norm, pair)
    return (pull_norm(grad_normed)[0], grad_w)

def product(form, first, second):
    return jnp.einsum(form, first.astype(jnp.float32), second.astype(jnp.float32), precision=HIGH)

def reference(pair, grad_out, w_in_out, w_out_out, w_in_in, w_out_in):
    normed_one, projected_one = prepare(pair, w_in_out)
    left_one, right_one, gate_one = gating(projected_one)
    mixed_one = product('ikh,jkh->ijh', left_one, right_one)
    pair_mid = finish(mixed_one, pair, gate_one, w_out_out)
    normed_two, projected_two = prepare(pair_mid, w_in_in)
    left_two, right_two, gate_two = gating(projected_two)
    mixed_two = product('kih,kjh->ijh', left_two, right_two)
    pair_new = finish(mixed_two, pair_mid, gate_two, w_out_in)
    grad_mixed_two, grad_gate_two, grad_wout_in = finish_back(grad_out, mixed_two, gate_two, w_out_in)
    grad_bf_two = grad_mixed_two.astype(jnp.bfloat16)
    grad_left_two = product('kjh,ijh->kih', right_two, grad_bf_two).astype(jnp.bfloat16)
    grad_right_two = product('kih,ijh->kjh', left_two, grad_bf_two).astype(jnp.bfloat16)
    grad_low_two, grad_win_in = prepare_back(pair_mid, normed_two, projected_two, grad_left_two, grad_right_two, grad_gate_two, w_in_in)
    grad_mid = grad_out + grad_low_two
    grad_mixed_one, grad_gate_one, grad_wout_out = finish_back(grad_mid, mixed_one, gate_one, w_out_out)
    grad_bf_one = grad_mixed_one.astype(jnp.bfloat16)
    grad_left_one = product('ijh,jkh->ikh', grad_bf_one, right_one).astype(jnp.bfloat16)
    grad_right_one = product('ijh,ikh->jkh', grad_bf_one, left_one).astype(jnp.bfloat16)
    grad_low_one, grad_win_out = prepare_back(pair, normed_one, projected_one, grad_left_one, grad_right_one, grad_gate_one, w_in_out)
    pair_grad = grad_mid + grad_low_one
    scale = 1.0 / N
    return (pair_new, pair_grad, grad_win_out * scale, grad_wout_out * scale, grad_win_in * scale, grad_wout_in * scale)
```

```python
import jax
import jax.numpy as jnp
from jax import lax
from jax.sharding import PartitionSpec as P

C = 128
EPS = 1e-05
BOTH = ("row", "col")
F32 = jnp.float32
BF16 = jnp.bfloat16


def norm_parts(values):
    center = values - jnp.mean(values, axis=-1, keepdims=True)
    rstd = lax.rsqrt(jnp.mean(center * center, axis=-1, keepdims=True) + EPS)
    return center * rstd, rstd


def norm_back(grad, normed, rstd):
    return rstd * (
        grad
        - jnp.mean(grad, axis=-1, keepdims=True)
        - normed * jnp.mean(grad * normed, axis=-1, keepdims=True)
    )


def exchange(x, axes):
    return lax.all_to_all(x, axes, 0, 0, tiled=True)


def matmul(a, b):
    return jnp.dot(a, b, preferred_element_type=F32)


class Sizes:
    def __init__(self, rows, cols, length, hidden):
        self.rows, self.cols = rows, cols
        self.n = length
        self.half = length // 2
        self.hidden = hidden


def to_channels(sz, left, right):
    def halves(x):
        return jnp.transpose(x, (2, 0, 1)).reshape(sz.hidden, 2, sz.half * sz.n)

    shape = (sz.hidden, 2, 2, sz.half * sz.n)
    l = jnp.broadcast_to(halves(left)[:, :, None], shape)
    r = jnp.broadcast_to(halves(right)[:, None, :], shape)
    sent = jnp.stack([l, r], axis=3).reshape(4 * sz.hidden, 2, sz.half * sz.n)
    return exchange(sent, BOTH)


def gather_pair(sz, got, kept_first):
    got = got.reshape(sz.rows, sz.cols, 2, sz.half, sz.n)
    if kept_first:
        got = jnp.transpose(got, (2, 0, 3, 1, 4))
    else:
        got = jnp.transpose(got, (2, 1, 3, 0, 4))
    return got.reshape(2, sz.half * sz.rows, sz.n * sz.cols)


def mix_out(sz, mixed):
    sent = mixed.astype(BF16).reshape(sz.rows, sz.half, sz.cols, sz.half)
    sent = jnp.transpose(sent, (0, 2, 1, 3)).reshape(sz.rows * sz.cols, 1, sz.half * sz.half)
    got = exchange(sent, BOTH).reshape(sz.hidden, 2, 2, sz.half, sz.half)
    return jnp.transpose(got, (1, 3, 2, 4, 0)).reshape(sz.n, sz.n, sz.hidden).astype(F32)


def mix_back_in(sz, grad):
    sent = grad.astype(BF16).reshape(2, sz.half, 2, sz.half, sz.hidden)
    sent = jnp.transpose(sent, (4, 0, 2, 1, 3)).reshape(4 * sz.hidden, 1, sz.half * sz.half)
    got = exchange(sent, BOTH).reshape(sz.rows, sz.cols, sz.half, sz.half)
    return jnp.transpose(got, (0, 2, 1, 3)).reshape(sz.rows * sz.half, sz.cols * sz.half)


def mix_back_out(sz, grads, kept_first):
    kept = sz.rows if kept_first else sz.cols
    other = sz.cols if kept_first else sz.rows
    sent = grads.astype(BF16).reshape(2, kept, sz.half, other, sz.n)
    sent = jnp.transpose(sent, (1, 3, 0, 2, 4) if kept_first else (3, 1, 0, 2, 4))
    sent = sent.reshape(sz.rows * sz.cols, 2, sz.half * sz.n)
    got = exchange(sent, BOTH).reshape(sz.hidden, 2, 2, 2, sz.half * sz.n).astype(F32)
    left = got[:, :, 0, 0] + got[:, :, 1, 0]
    right = got[:, 0, :, 1] + got[:, 1, :, 1]

    def back(x):
        return jnp.transpose(x.reshape(sz.hidden, sz.n, sz.n), (1, 2, 0))

    return back(left), back(right)


def channel_grads(pair, grad):
    grad_left = matmul(grad, pair[1])
    grad_right = lax.dot_general(
        grad, pair[0], (((0,), (0,)), ((), ())), preferred_element_type=F32
    )
    return jnp.stack([grad_left, grad_right])


def everywhere(sz, x):
    flat = x.reshape(sz.rows, -1, C)
    got = exchange(flat, "row")
    part = jnp.sum(got, axis=0)
    spread = jnp.broadcast_to(part[None], (sz.cols,) + part.shape)
    part = jnp.sum(exchange(spread, "col"), axis=0)
    spread = jnp.broadcast_to(part[None], (sz.rows,) + part.shape)
    return exchange(spread, "row").reshape(x.shape)


def prepare(pair, w_in, hidden):
    normed, rstd = norm_parts(pair)
    low = normed.astype(BF16)
    projected = matmul(low, w_in)
    a, ag, b, bg = (projected[..., i * hidden : (i + 1) * hidden] for i in range(4))
    sa, sb = jax.nn.sigmoid(ag), jax.nn.sigmoid(bg)
    gate = jax.nn.sigmoid(projected[..., 4 * hidden :])
    return normed, rstd, low, (a, sa, b, sb), gate


def prepare_back(normed, rstd, low, parts, gate, w_in, grad_left, grad_right, grad_gate):
    a, sa, b, sb = parts
    grad_projected = jnp.concatenate(
        [
            grad_left * sa,
            grad_left * a * sa * (1 - sa),
            grad_right * sb,
            grad_right * b * sb * (1 - sb),
            grad_gate * gate * (1 - gate),
        ],
        axis=-1,
    ).astype(BF16)
    grad_w = lax.dot_general(
        low, grad_projected, (((0, 1), (0, 1)), ((), ())), preferred_element_type=F32
    )
    grad_normed = lax.dot_general(
        grad_projected, w_in, (((2,), (1,)), ((), ())), preferred_element_type=F32
    )
    return norm_back(grad_normed, normed, rstd), grad_w


def finish(mixed, pair, gate, w_out):
    normed, rstd = norm_parts(mixed)
    post = normed.astype(BF16)
    projected = matmul(post, w_out)
    return pair + gate * projected, (normed, rstd, post, projected)


def finish_back(grad_new, kept, gate, w_out):
    normed, rstd, post, projected = kept
    grad_gate = grad_new * projected
    grad_proj = (grad_new * gate).astype(BF16)
    grad_w = lax.dot_general(
        post, grad_proj, (((0, 1), (0, 1)), ((), ())), preferred_element_type=F32
    )
    grad_post = lax.dot_general(
        grad_proj, w_out, (((2,), (1,)), ((), ())), preferred_element_type=F32
    )
    return norm_back(grad_post, normed, rstd), grad_gate, grad_w


def swap(x):
    return jnp.swapaxes(x, 0, 1)


def local(pair, grad_out, w_in_out, w_out_out, w_in_in, w_out_in):
    hidden = w_out_out.shape[0]
    sz = Sizes(lax.axis_size("row"), lax.axis_size("col"), pair.shape[0], hidden)

    normed1, rstd1, low1, parts1, gate1 = prepare(pair, w_in_out, hidden)
    a, sa, b, sb = parts1
    pair1 = gather_pair(sz, to_channels(sz, (sa * a).astype(BF16), (sb * b).astype(BF16)), True)
    mixed1 = mix_out(sz, matmul(pair1[0], pair1[1].T))
    mid, kept1 = finish(mixed1, pair, gate1, w_out_out)

    normed2, rstd2, low2, parts2, gate2 = prepare(mid, w_in_in, hidden)
    a, sa, b, sb = parts2
    pair2 = gather_pair(
        sz, to_channels(sz, swap((sa * a).astype(BF16)), swap((sb * b).astype(BF16))), False
    )
    mixed2 = mix_out(sz, matmul(pair2[0], pair2[1].T))
    pair_new, kept2 = finish(mixed2, mid, gate2, w_out_in)

    grad_mixed2, grad_gate2, grad_wout_in = finish_back(grad_out, kept2, gate2, w_out_in)
    grad_left2, grad_right2 = mix_back_out(
        sz, channel_grads(pair2, mix_back_in(sz, grad_mixed2)), False
    )
    low_grad2, grad_win_in = prepare_back(
        normed2, rstd2, low2, parts2, gate2, w_in_in, swap(grad_left2), swap(grad_right2), grad_gate2
    )
    grad_mid = grad_out + low_grad2

    grad_mixed1, grad_gate1, grad_wout_out = finish_back(grad_mid, kept1, gate1, w_out_out)
    grad_left1, grad_right1 = mix_back_out(
        sz, channel_grads(pair1, mix_back_in(sz, grad_mixed1)), True
    )
    low_grad1, grad_win_out = prepare_back(
        normed1, rstd1, low1, parts1, gate1, w_in_out, grad_left1, grad_right1, grad_gate1
    )
    pair_grad = grad_mid + low_grad1

    weights = [grad_win_out, grad_wout_out, grad_win_in, grad_wout_in]
    flat = jnp.concatenate([w.reshape(-1) for w in weights]) * (1.0 / (sz.n * sz.rows))
    flat = everywhere(sz, flat)
    outs, at = [], 0
    for w in weights:
        outs.append(flat[at : at + w.size].reshape(w.shape))
        at += w.size
    return (pair_new, pair_grad, *outs)


def solution(mesh):
    placed = (P("row", "col", None), P("row", "col", None), P(), P(), P(), P())
    return jax.shard_map(
        local,
        mesh=mesh,
        in_specs=placed,
        out_specs=(P("row", "col", None), P("row", "col", None), P(), P(), P(), P()),
        check_vma=False,
    )
```

```python
import functools

import jax
import jax.numpy as jnp
import numpy as np
from jax import lax
from jax.experimental import pallas as pl
from jax.experimental.pallas import tpu as pltpu
from jax.sharding import Mesh
from jax.sharding import PartitionSpec as P

EPS = 1e-05
F32 = jnp.float32
BF16 = jnp.bfloat16
PARTS = 4
ROW = ("row_hi", "row_lo")
COL = ("col_hi", "col_lo")


def dot(a, b, ca, cb):
    return lax.dot_general(a, b, (((ca,), (cb,)), ((), ())), preferred_element_type=F32)


def norm(x):
    center = x - jnp.mean(x, axis=0, keepdims=True)
    rstd = lax.rsqrt(jnp.mean(center * center, axis=0, keepdims=True) + EPS)
    return center * rstd, rstd


def norm_back(grad, normed, rstd):
    return rstd * (
        grad
        - jnp.mean(grad, axis=0, keepdims=True)
        - normed * jnp.mean(grad * normed, axis=0, keepdims=True)
    )


def swap_cells(ref, n):
    return jnp.concatenate([ref[pl.ds(j, n, stride=n), :] for j in range(n)], axis=0)


def project(x, w_in, proj_ref, left_ref, right_ref):
    h = left_ref.shape[0]
    normed, _ = norm(x)
    proj = dot(w_in, normed.astype(BF16), 0, 0)
    proj_ref[...] = proj
    left_ref[...] = (jax.nn.sigmoid(proj[h : 2 * h]) * proj[:h]).astype(BF16)
    right_ref[...] = (jax.nn.sigmoid(proj[3 * h : 4 * h]) * proj[2 * h : 3 * h]).astype(BF16)


def project_back(x, proj_ref, w_in, gl, gr, grad_gate, grad_w_ref):
    h = gl.shape[0]
    normed, rstd = norm(x)
    sa = jax.nn.sigmoid(proj_ref[h : 2 * h, :])
    sb = jax.nn.sigmoid(proj_ref[3 * h : 4 * h, :])
    gate = jax.nn.sigmoid(proj_ref[4 * h :, :])
    gla, grb = gl * sa, gr * sb
    grad = jnp.concatenate(
        [
            gla,
            gla * proj_ref[:h, :] * (1 - sa),
            grb,
            grb * proj_ref[2 * h : 3 * h, :] * (1 - sb),
            grad_gate * gate * (1 - gate),
        ],
        axis=0,
    ).astype(BF16)
    low = normed.astype(BF16)
    c = x.shape[0]
    for at in range(0, grad.shape[0], c):
        grad_w_ref[at : at + c, :] = dot(low, grad[at : at + c], 1, 1)
    return norm_back(dot(w_in, grad, 1, 0), normed, rstd)


def finish(mixed, w_out):
    normed, rstd = norm(mixed)
    post = normed.astype(BF16)
    return dot(w_out, post, 0, 0), normed, rstd, post


def finish_back(grad_new, gate, out, normed, rstd, post, w_out):
    grad_gate = grad_new * out
    grad_proj = (grad_new * gate).astype(BF16)
    grad_w = dot(post, grad_proj, 1, 1)
    return norm_back(dot(w_out, grad_proj, 1, 0), normed, rstd), grad_gate, grad_w


def summed(lo_ref, hi_ref):
    def total(ref):
        parts = [ref[q].astype(F32) for q in range(PARTS)]
        return (parts[0] + parts[1]) + (parts[2] + parts[3])

    return jnp.concatenate([total(lo_ref), total(hi_ref)], axis=1)


def start_one(pair_ref, w_ref, left_ref, right_ref, proj_ref, pair_t_ref):
    x = pair_ref[...].T
    pair_t_ref[...] = x
    project(x, w_ref[...], proj_ref, left_ref, right_ref)


def middle(
    lo_ref, hi_ref, pair_t_ref, proj1_ref, w_out_ref, w_in_ref,
    left_ref, right_ref, proj2_ref, mixed_ref, mid_ref, scratch,
):
    h = left_ref.shape[0]
    mixed = summed(lo_ref, hi_ref)
    mixed_ref[...] = mixed
    out, *_ = finish(mixed, w_out_ref[...])
    mid = pair_t_ref[...] + jax.nn.sigmoid(proj1_ref[4 * h :, :]) * out
    scratch[...] = mid.T
    mid = swap_cells(scratch, int(round(scratch.shape[0] ** 0.5))).T
    mid_ref[...] = mid
    project(mid, w_in_ref[...], proj2_ref, left_ref, right_ref)


def turn(
    lo_ref, hi_ref, mid_ref, proj_ref, grad_out_ref, w_out_ref,
    new_ref, grad_ref, grad_gate_ref, grad_w_ref, scratch,
):
    h = grad_ref.shape[0]
    n = new_ref.shape[0]
    out, normed, rstd, post = finish(summed(lo_ref, hi_ref), w_out_ref[...])
    gate = jax.nn.sigmoid(proj_ref[4 * h :, :])
    new = (mid_ref[...] + gate * out).T
    scratch[...] = new
    new_ref[...] = swap_cells(scratch, n).reshape(new_ref.shape)
    grad_new = swap_cells(grad_out_ref, n).T
    grad, grad_gate, grad_w = finish_back(grad_new, gate, out, normed, rstd, post, w_out_ref[...])
    grad_ref[...] = grad.astype(BF16)
    grad_gate_ref[...] = grad_gate
    grad_w_ref[...] = grad_w


def between(
    gl_ref, gr_ref, mid_ref, proj2_ref, grad_gate2_ref, w_in_ref, grad_out_ref, mixed_ref, proj1_ref, w_out_ref,
    grad_ref, grad_gate_ref, grad_mid_ref, grad_win_ref, grad_wout_ref, scratch,
):
    h = grad_ref.shape[0]
    low = project_back(
        mid_ref[...], proj2_ref, w_in_ref[...], gl_ref[...].astype(F32), gr_ref[...].astype(F32),
        grad_gate2_ref[...], grad_win_ref,
    )
    scratch[...] = low.T
    n = int(round(scratch.shape[0] ** 0.5))
    grad_mid = (grad_out_ref[...] + swap_cells(scratch, n)).T
    grad_mid_ref[...] = grad_mid
    w_out = w_out_ref[...]
    out, normed, rstd, post = finish(mixed_ref[...], w_out)
    gate = jax.nn.sigmoid(proj1_ref[4 * h :, :])
    grad, grad_gate, grad_w = finish_back(grad_mid, gate, out, normed, rstd, post, w_out)
    grad_ref[...] = grad.astype(BF16)
    grad_gate_ref[...] = grad_gate
    grad_wout_ref[...] = grad_w


def last(
    gl_ref, gr_ref, pair_t_ref, proj_ref, grad_gate_ref, w_in_ref, grad_mid_ref, win2_ref, wout2_ref, wout1_ref,
    pair_grad_ref, weights_ref, scratch,
):
    low = project_back(
        pair_t_ref[...], proj_ref, w_in_ref[...], gl_ref[...].astype(F32), gr_ref[...].astype(F32),
        grad_gate_ref[...], scratch,
    )
    pair_grad_ref[...] = (grad_mid_ref[...] + low).T
    weights_ref[...] = jnp.concatenate(
        [scratch[...], wout1_ref[...], win2_ref[...], wout2_ref[...]], axis=0
    ).astype(BF16)


def blocks(x, outer, inner, size, wide):
    rows = []
    for r in range(inner):
        rows.append(
            jnp.concatenate(
                [x[o * size : (o + 1) * size, r * wide : (r + 1) * wide] for o in range(outer)], axis=1
            )
        )
    return jnp.concatenate(rows, axis=0)


def reorder(ref, outer, inner):
    return jnp.concatenate([ref[pl.ds(r, outer, stride=inner), :] for r in range(inner)], axis=0)


def multiply(size, wide, first_ref, second_ref, lo_ref, hi_ref, first_out_ref, second_out_ref, scratch):
    part = first_ref.shape[0] // size
    first = blocks(first_ref[...].astype(F32), part, wide, size, wide).astype(BF16)
    scratch[...] = blocks(second_ref[...].astype(F32), part, wide, size, wide)
    second = reorder(scratch, wide, size).astype(BF16)
    first_out_ref[...] = first
    second_out_ref[...] = second
    out = blocks(dot(first, second, 1, 1), wide, size, size, wide).astype(BF16)
    half = lo_ref.shape[1]
    lo_ref[...] = out[:, :half]
    hi_ref[...] = out[:, half:]


def multiply_back(size, wide, lo_ref, hi_ref, first_ref, second_ref, gf_ref, gs_ref, scratch):
    part = gf_ref.shape[0] // size
    got = jnp.concatenate([lo_ref[...].astype(F32), hi_ref[...].astype(F32)], axis=1)
    grad = blocks(got, size, wide, size, wide).astype(BF16)
    gf_ref[...] = blocks(dot(grad, second_ref[...], 1, 0), wide, part, size, wide).astype(BF16)
    scratch[...] = dot(grad, first_ref[...], 0, 0)
    gs_ref[...] = blocks(reorder(scratch, size, wide), wide, part, size, wide).astype(BF16)


def call(body, outs, *args, scratch=None):
    return pl.pallas_call(
        body,
        out_shape=[jax.ShapeDtypeStruct(s, t) for s, t in outs],
        scratch_shapes=[] if scratch is None else [pltpu.VMEM(scratch, F32)],
        compiler_params=pltpu.CompilerParams(vmem_limit_bytes=48 * 1024 * 1024),
    )(*args)


def exchange(x, axes):
    return lax.all_to_all(x, axes, 0, 0, tiled=True)


def local(pair, grad_out, w_in_out, w_out_out, w_in_in, w_out_in):
    n, _, c = pair.shape
    h = w_out_out.shape[0]
    wide = w_in_out.shape[1]
    size = lax.axis_size(ROW)
    cells = n * n
    half = cells // 2
    part = size // PARTS
    low = (h, cells)
    k_shape = (size * n, part * n)
    pair = pair.reshape(cells, c)
    grad_out = grad_out.reshape(cells, c)

    def apart(first, second, axes):
        got = exchange(jnp.stack([first, second], axis=1), axes)
        return got[:, 0], got[:, 1]

    def product(first, second, group, everyone):
        first, second = apart(first, second, group)
        lo, hi, first, second = call(
            functools.partial(multiply, size, n),
            [((size * size, half), BF16), ((size * size, half), BF16), (k_shape, BF16), (k_shape, BF16)],
            first, second, scratch=k_shape,
        )
        lo, hi = apart(lo, hi, everyone)
        return lo.reshape(PARTS, h, half), hi.reshape(PARTS, h, half), first, second

    def product_back(grad, first, second, group, everyone):
        sent = jnp.broadcast_to(grad.reshape(1, h, 2, half), (PARTS, h, 2, half)).reshape(PARTS * h, 2, half)
        got = exchange(sent, everyone)
        gf, gs = call(
            functools.partial(multiply_back, size, n), [(low, BF16), (low, BF16)],
            got[:, 0], got[:, 1], first, second, scratch=k_shape,
        )
        return apart(gf, gs, group)

    one = (("col_lo",) + ROW, COL + ROW)
    two = (("row_lo",) + COL, ROW + COL)

    left1, right1, proj1, pair_t = call(
        start_one, [(low, BF16), (low, BF16), ((wide, cells), F32), ((c, cells), F32)], pair, w_in_out
    )
    lo, hi, first1, second1 = product(left1, right1, *one)
    left2, right2, proj2, mixed1, mid_t = call(
        middle,
        [(low, BF16), (low, BF16), ((wide, cells), F32), (low, F32), ((c, cells), F32)],
        lo, hi, pair_t, proj1, w_out_out, w_in_in, scratch=(cells, c),
    )
    lo, hi, first2, second2 = product(right2, left2, *two)
    pair_new, grad2, grad_gate2, grad_wout_in = call(
        turn,
        [((n, n, c), F32), (low, BF16), ((c, cells), F32), ((h, c), F32)],
        lo, hi, mid_t, proj2, grad_out, w_out_in, scratch=(cells, c),
    )
    gr2, gl2 = product_back(grad2, first2, second2, *two)
    grad1, grad_gate1, grad_mid, grad_win_in, grad_wout_out = call(
        between,
        [(low, BF16), ((c, cells), F32), ((c, cells), F32), ((wide, c), F32), ((h, c), F32)],
        gl2, gr2, mid_t, proj2, grad_gate2, w_in_in, grad_out, mixed1, proj1, w_out_out, scratch=(cells, c),
    )
    gl1, gr1 = product_back(grad1, first1, second1, *one)
    weight_rows = 2 * (wide + h)
    pair_grad, weights = call(
        last,
        [((cells, c), F32), ((weight_rows, c), BF16)],
        gl1, gr1, pair_t, proj1, grad_gate1, w_in_out, grad_mid, grad_win_in, grad_wout_in, grad_wout_out,
        scratch=(wide, c),
    )

    each = weight_rows // size
    part_sum = jnp.sum(exchange(weights.reshape(size, each, c), ROW).astype(F32), axis=0)
    spread = jnp.broadcast_to(part_sum.astype(BF16)[None], (size, each, c))
    total = jnp.sum(exchange(spread, COL).astype(F32), axis=0) * (1.0 / (n * size))
    spread = jnp.broadcast_to(total.astype(BF16)[None], (size, each, c))
    weights = exchange(spread, ROW).reshape(weight_rows, c).astype(F32)

    def columns(x):
        return jnp.concatenate([x[at : at + c] for at in range(0, wide, c)], axis=1)

    at = wide + h
    return (
        pair_new,
        pair_grad.reshape(n, n, c),
        columns(weights[:wide]),
        weights[wide:at],
        columns(weights[at : at + wide]),
        weights[at + wide :],
    )


def solution(mesh):
    rows, cols = mesh.devices.shape
    fine = Mesh(mesh.devices.reshape(PARTS, rows // PARTS, PARTS, cols // PARTS), ROW + COL)
    cell = P(ROW, COL, None)
    return jax.shard_map(
        local,
        mesh=fine,
        in_specs=(cell, cell, P(), P(), P(), P()),
        out_specs=(cell, cell, P(), P(), P(), P()),
        check_vma=False,
    )
```

```python
import functools

import jax
import jax.numpy as jnp
import numpy as np
from jax import lax
from jax.experimental import pallas as pl
from jax.experimental.pallas import tpu as pltpu
from jax.sharding import Mesh
from jax.sharding import PartitionSpec as P

EPS = 1e-05
F32 = jnp.float32
BF16 = jnp.bfloat16
PARTS = 4
ROW = ("row_hi", "row_lo")
COL = ("col_y", "col_hi", "col_lo")
NEAR = ROW + ("col_y",)
FAR = ("col_hi", "col_lo")


def dot(a, b, ca, cb):
    return lax.dot_general(a, b, (((ca,), (cb,)), ((), ())), preferred_element_type=F32)


def norm(x):
    center = x - jnp.mean(x, axis=0, keepdims=True)
    rstd = lax.rsqrt(jnp.mean(center * center, axis=0, keepdims=True) + EPS)
    return center * rstd, rstd


def norm_back(grad, normed, rstd):
    return rstd * (
        grad
        - jnp.mean(grad, axis=0, keepdims=True)
        - normed * jnp.mean(grad * normed, axis=0, keepdims=True)
    )


def swap_cells(ref, n):
    return jnp.concatenate([ref[pl.ds(j, n, stride=n), :] for j in range(n)], axis=0)


def project(x, w_in, proj_ref, sent_ref, order):
    h = sent_ref.shape[0]
    normed, _ = norm(x)
    proj = dot(w_in, normed.astype(BF16), 0, 0)
    proj_ref[...] = proj
    for at, place in zip((0, 2 * h), order):
        gated = jax.nn.sigmoid(proj[at + h : at + 2 * h]) * proj[at : at + h]
        sent_ref[:, place, :] = gated.astype(BF16)


def project_back(x, proj_ref, w_in, gl, gr, grad_gate, grad_w_ref):
    h = gl.shape[0]
    normed, rstd = norm(x)
    sa = jax.nn.sigmoid(proj_ref[h : 2 * h, :])
    sb = jax.nn.sigmoid(proj_ref[3 * h : 4 * h, :])
    gate = jax.nn.sigmoid(proj_ref[4 * h :, :])
    gla, grb = gl * sa, gr * sb
    grad = jnp.concatenate(
        [
            gla,
            gla * proj_ref[:h, :] * (1 - sa),
            grb,
            grb * proj_ref[2 * h : 3 * h, :] * (1 - sb),
            grad_gate * gate * (1 - gate),
        ],
        axis=0,
    ).astype(BF16)
    low = normed.astype(BF16)
    c = x.shape[0]
    for at in range(0, grad.shape[0], c):
        grad_w_ref[at : at + c, :] = dot(low, grad[at : at + c], 1, 1)
    return norm_back(dot(w_in, grad, 1, 0), normed, rstd)


def finish(mixed, w_out):
    normed, rstd = norm(mixed)
    post = normed.astype(BF16)
    return dot(w_out, post, 0, 0), normed, rstd, post


def finish_back(grad_new, gate, out, normed, rstd, post, w_out):
    grad_gate = grad_new * out
    grad_proj = (grad_new * gate).astype(BF16)
    grad_w = dot(post, grad_proj, 1, 1)
    return norm_back(dot(w_out, grad_proj, 1, 0), normed, rstd), grad_gate, grad_w


def summed(got_ref):
    h = got_ref.shape[0] // PARTS

    def total(k):
        parts = [got_ref[q * h : (q + 1) * h, k, :].astype(F32) for q in range(PARTS)]
        return (parts[0] + parts[1]) + (parts[2] + parts[3])

    return jnp.concatenate([total(0), total(1)], axis=1)


def send_halves(x, sent_ref):
    half = sent_ref.shape[2]
    for at in range(0, sent_ref.shape[0], x.shape[0]):
        sent_ref[at : at + x.shape[0], 0, :] = x[:, :half]
        sent_ref[at : at + x.shape[0], 1, :] = x[:, half:]


def start_one(pair_ref, w_ref, sent_ref, proj_ref, pair_t_ref):
    x = pair_ref[...].T
    pair_t_ref[...] = x
    project(x, w_ref[...], proj_ref, sent_ref, (0, 1))


def middle(
    got_ref, pair_t_ref, proj1_ref, w_out_ref, w_in_ref,
    sent_ref, proj2_ref, mixed_ref, mid_ref, scratch,
):
    h = sent_ref.shape[0]
    mixed = summed(got_ref)
    mixed_ref[...] = mixed
    out, *_ = finish(mixed, w_out_ref[...])
    mid = pair_t_ref[...] + jax.nn.sigmoid(proj1_ref[4 * h :, :]) * out
    scratch[...] = mid.T
    mid = swap_cells(scratch, int(round(scratch.shape[0] ** 0.5))).T
    mid_ref[...] = mid
    project(mid, w_in_ref[...], proj2_ref, sent_ref, (1, 0))


def turn(
    got_ref, mid_ref, proj_ref, grad_out_ref, w_out_ref,
    new_ref, sent_ref, grad_gate_ref, grad_w_ref, scratch,
):
    h = got_ref.shape[0] // PARTS
    n = new_ref.shape[0]
    out, normed, rstd, post = finish(summed(got_ref), w_out_ref[...])
    gate = jax.nn.sigmoid(proj_ref[4 * h :, :])
    new = (mid_ref[...] + gate * out).T
    scratch[...] = new
    new_ref[...] = swap_cells(scratch, n).reshape(new_ref.shape)
    grad_new = swap_cells(grad_out_ref, n).T
    grad, grad_gate, grad_w = finish_back(grad_new, gate, out, normed, rstd, post, w_out_ref[...])
    send_halves(grad.astype(BF16), sent_ref)
    grad_gate_ref[...] = grad_gate
    grad_w_ref[...] = grad_w


def between(
    got_ref, mid_ref, proj2_ref, grad_gate2_ref, w_in_ref, grad_out_ref, mixed_ref, proj1_ref, w_out_ref,
    sent_ref, grad_gate_ref, grad_mid_ref, grad_win_ref, grad_wout_ref, scratch,
):
    h = got_ref.shape[0]
    low = project_back(
        mid_ref[...], proj2_ref, w_in_ref[...], got_ref[:, 1, :].astype(F32), got_ref[:, 0, :].astype(F32),
        grad_gate2_ref[...], grad_win_ref,
    )
    scratch[...] = low.T
    n = int(round(scratch.shape[0] ** 0.5))
    grad_mid = (grad_out_ref[...] + swap_cells(scratch, n)).T
    grad_mid_ref[...] = grad_mid
    w_out = w_out_ref[...]
    out, normed, rstd, post = finish(mixed_ref[...], w_out)
    gate = jax.nn.sigmoid(proj1_ref[4 * h :, :])
    grad, grad_gate, grad_w = finish_back(grad_mid, gate, out, normed, rstd, post, w_out)
    send_halves(grad.astype(BF16), sent_ref)
    grad_gate_ref[...] = grad_gate
    grad_wout_ref[...] = grad_w


def last(
    got_ref, pair_t_ref, proj_ref, grad_gate_ref, w_in_ref, grad_mid_ref, win2_ref, wout2_ref, wout1_ref,
    pair_grad_ref, weights_ref, scratch,
):
    low = project_back(
        pair_t_ref[...], proj_ref, w_in_ref[...], got_ref[:, 0, :].astype(F32), got_ref[:, 1, :].astype(F32),
        grad_gate_ref[...], scratch,
    )
    pair_grad_ref[...] = (grad_mid_ref[...] + low).T
    weights_ref[...] = jnp.concatenate(
        [scratch[...], wout1_ref[...], win2_ref[...], wout2_ref[...]], axis=0
    ).astype(BF16)


def blocks(x, outer, inner, size, wide):
    rows = []
    for r in range(inner):
        rows.append(
            jnp.concatenate(
                [x[o * size : (o + 1) * size, r * wide : (r + 1) * wide] for o in range(outer)], axis=1
            )
        )
    return jnp.concatenate(rows, axis=0)


def reorder(ref, outer, inner):
    return jnp.concatenate([ref[pl.ds(r, outer, stride=inner), :] for r in range(inner)], axis=0)


def multiply(size, wide, got_ref, sent_ref, first_out_ref, second_out_ref, scratch):
    part = got_ref.shape[0] // size
    first = blocks(got_ref[:, 0, :].astype(F32), part, wide, size, wide).astype(BF16)
    scratch[...] = blocks(got_ref[:, 1, :].astype(F32), part, wide, size, wide)
    second = reorder(scratch, wide, size).astype(BF16)
    first_out_ref[...] = first
    second_out_ref[...] = second
    out = blocks(dot(first, second, 1, 1), wide, size, size, wide).astype(BF16)
    send_halves(out, sent_ref)


def multiply_back(size, wide, got_ref, first_ref, second_ref, sent_ref, scratch):
    part = sent_ref.shape[0] // size
    got = jnp.concatenate([got_ref[:, 0, :].astype(F32), got_ref[:, 1, :].astype(F32)], axis=1)
    grad = blocks(got, size, wide, size, wide).astype(BF16)
    sent_ref[:, 0, :] = blocks(dot(grad, second_ref[...], 1, 0), wide, part, size, wide).astype(BF16)
    scratch[...] = dot(grad, first_ref[...], 0, 0)
    sent_ref[:, 1, :] = blocks(reorder(scratch, size, wide), wide, part, size, wide).astype(BF16)


def sum_and_spread(got_ref, sent_ref):
    total = got_ref[0].astype(F32)
    for i in range(1, got_ref.shape[0]):
        total += got_ref[i].astype(F32)
    total = total.astype(BF16)
    for i in range(sent_ref.shape[0]):
        sent_ref[i] = total


def unpack(scale, got_ref, *out_refs):
    at = 0
    for ref in out_refs:
        c = got_ref.shape[1]
        rows = ref.shape[0]
        for lane in range(0, ref.shape[1], c):
            ref[:, lane : lane + c] = got_ref[at : at + rows, :].astype(F32) * scale
            at += rows


def call(body, outs, *args, scratch=None):
    return pl.pallas_call(
        body,
        out_shape=[jax.ShapeDtypeStruct(s, t) for s, t in outs],
        scratch_shapes=[] if scratch is None else [pltpu.VMEM(scratch, F32)],
        compiler_params=pltpu.CompilerParams(vmem_limit_bytes=16 * 1024 * 1024),
    )(*args)


def exchange(x, axes):
    return lax.all_to_all(x, axes, 0, 0, tiled=True)


def local(pair, grad_out, w_in_out, w_out_out, w_in_in, w_out_in):
    n, _, c = pair.shape
    h = w_out_out.shape[0]
    wide = w_in_out.shape[1]
    size = lax.axis_size(ROW)
    cells = n * n
    part = size // PARTS
    low = (h, cells)
    k_shape = (size * n, part * n)
    pair = pair.reshape(cells, c)
    grad_out = grad_out.reshape(cells, c)

    cell_array = ((c, cells), F32)
    near = ((h, 2, cells), BF16)
    all_devices = ((size * size, 2, cells // 2), BF16)

    def product(sent, group, everyone):
        sent, first, second = call(
            functools.partial(multiply, size, n),
            [all_devices, (k_shape, BF16), (k_shape, BF16)],
            exchange(sent, group), scratch=k_shape,
        )
        return exchange(sent, everyone), first, second

    def product_back(sent, first, second, group, everyone):
        sent, = call(
            functools.partial(multiply_back, size, n), [near], exchange(sent, everyone), first, second, scratch=k_shape
        )
        return exchange(sent, group)

    one = (("col_lo",) + ROW, COL + ROW)
    two = (("row_lo",) + COL, ROW + COL)

    sent, proj1, pair_t = call(start_one, [near, ((wide, cells), F32), cell_array], pair, w_in_out)
    got, first1, second1 = product(sent, *one)
    sent, proj2, mixed1, mid_t = call(
        middle,
        [near, ((wide, cells), F32), (low, F32), cell_array],
        got, pair_t, proj1, w_out_out, w_in_in, scratch=(cells, c),
    )
    got, first2, second2 = product(sent, *two)
    pair_new, sent, grad_gate2, grad_wout_in = call(
        turn,
        [((n, n, c), F32), all_devices, cell_array, ((h, c), F32)],
        got, mid_t, proj2, grad_out, w_out_in, scratch=(cells, c),
    )
    got = product_back(sent, first2, second2, *two)
    sent, grad_gate1, grad_mid, grad_win_in, grad_wout_out = call(
        between,
        [all_devices, cell_array, cell_array, ((wide, c), F32), ((h, c), F32)],
        got, mid_t, proj2, grad_gate2, w_in_in, grad_out, mixed1, proj1, w_out_out, scratch=(cells, c),
    )
    got = product_back(sent, first1, second1, *one)
    weight_rows = 2 * (wide + h)
    pair_grad, weights = call(
        last,
        [((cells, c), F32), ((weight_rows, c), BF16)],
        got, pair_t, proj1, grad_gate1, w_in_out, grad_mid, grad_win_in, grad_wout_in, grad_wout_out,
        scratch=(wide, c),
    )

    near_count, far_count = lax.axis_size(NEAR), lax.axis_size(FAR)
    each = weight_rows // near_count
    got = exchange(weights.reshape(near_count, each, c), NEAR)
    sent, = call(sum_and_spread, [((far_count, each, c), BF16)], got)
    sent, = call(sum_and_spread, [((near_count, each, c), BF16)], exchange(sent, FAR))
    outs = call(
        functools.partial(unpack, 1.0 / (n * size)),
        [((c, wide), F32), ((h, c), F32), ((c, wide), F32), ((h, c), F32)],
        exchange(sent, NEAR).reshape(weight_rows, c),
    )
    return (pair_new, pair_grad.reshape(n, n, c), *outs)


def solution(mesh):
    rows, cols = mesh.devices.shape
    fine = Mesh(mesh.devices.reshape(PARTS, rows // PARTS, 2, PARTS // 2, cols // PARTS), ROW + COL)
    cell = P(ROW, COL, None)
    return jax.shard_map(
        local,
        mesh=fine,
        in_specs=(cell, cell, P(), P(), P(), P()),
        out_specs=(cell, cell, P(), P(), P(), P()),
        check_vma=False,
    )
```

```python
import functools

import jax
import jax.numpy as jnp
from jax import lax
from jax.experimental import pallas as pl
from jax.experimental.pallas import tpu as pltpu
from jax.sharding import Mesh
from jax.sharding import PartitionSpec as P

EPS = 1e-05
F32 = jnp.float32
BF16 = jnp.bfloat16
PARTS = 4
SPLIT = 2
ROW = ("row_a", "row_q", "row_b")
COL = ("col_a", "col_q", "col_b")
NEAR = ("col_a",) + ROW
FAR = ("col_q", "col_b")


def dot(a, b, ca, cb):
    return lax.dot_general(a, b, (((ca,), (cb,)), ((), ())), preferred_element_type=F32)


def norm(x):
    center = x - jnp.mean(x, axis=0, keepdims=True)
    rstd = lax.rsqrt(jnp.mean(center * center, axis=0, keepdims=True) + EPS)
    return center * rstd, rstd


def norm_back(grad, normed, rstd):
    return rstd * (
        grad
        - jnp.mean(grad, axis=0, keepdims=True)
        - normed * jnp.mean(grad * normed, axis=0, keepdims=True)
    )


def swap_cells(ref, n):
    return jnp.concatenate([ref[pl.ds(j, n, stride=n), :] for j in range(n)], axis=0)


def project(x, w_in, proj_ref, sent_ref, order):
    h = sent_ref.shape[0]
    normed, _ = norm(x)
    proj = dot(w_in, normed.astype(BF16), 0, 0)
    proj_ref[...] = proj
    for at, place in zip((0, 2 * h), order):
        gated = jax.nn.sigmoid(proj[at + h : at + 2 * h]) * proj[at : at + h]
        sent_ref[:, place, :] = gated.astype(BF16)


def project_back(x, proj_ref, w_in, gl, gr, grad_gate):
    h = gl.shape[0]
    normed, rstd = norm(x)
    sa = jax.nn.sigmoid(proj_ref[h : 2 * h, :])
    sb = jax.nn.sigmoid(proj_ref[3 * h : 4 * h, :])
    gate = jax.nn.sigmoid(proj_ref[4 * h :, :])
    gla, grb = gl * sa, gr * sb
    grad = jnp.concatenate(
        [
            gla,
            gla * proj_ref[:h, :] * (1 - sa),
            grb,
            grb * proj_ref[2 * h : 3 * h, :] * (1 - sb),
            grad_gate * gate * (1 - gate),
        ],
        axis=0,
    ).astype(BF16)
    return norm_back(dot(w_in, grad, 1, 0), normed, rstd), normed.astype(BF16), grad


def finish(mixed, w_out):
    normed, rstd = norm(mixed)
    post = normed.astype(BF16)
    return dot(w_out, post, 0, 0), normed, rstd, post


def finish_back(grad_new, gate, out, normed, rstd, post, w_out):
    grad_gate = grad_new * out
    grad_proj = (grad_new * gate).astype(BF16)
    grad_w = dot(post, grad_proj, 1, 1)
    return norm_back(dot(w_out, grad_proj, 1, 0), normed, rstd), grad_gate, grad_w


def owners(count, h):
    run = h // SPLIT
    return [(at, (at // run // PARTS) * run, run) for at in range(0, count, run)]


def summed(got_ref):
    count = got_ref.shape[0]
    h = count // PARTS

    def total(k):
        sums = {}
        for at, channel, run in owners(count, h):
            part = got_ref[at : at + run, k, :].astype(F32)
            sums[channel] = sums[channel] + part if channel in sums else part
        return jnp.concatenate(list(sums.values()), axis=0)

    return jnp.concatenate([total(0), total(1)], axis=1)


def start_one(pair_ref, w_ref, sent_ref, proj_ref, pair_t_ref):
    x = pair_ref[...].T
    pair_t_ref[...] = x
    project(x, w_ref[...], proj_ref, sent_ref, (0, 1))


def middle(
    got_ref, pair_t_ref, proj1_ref, w_out_ref, w_in_ref,
    sent_ref, proj2_ref, mixed_ref, mid_ref, scratch,
):
    h = sent_ref.shape[0]
    mixed = summed(got_ref)
    mixed_ref[...] = mixed
    out, *_ = finish(mixed, w_out_ref[...])
    mid = pair_t_ref[...] + jax.nn.sigmoid(proj1_ref[4 * h :, :]) * out
    scratch[...] = mid.T
    mid = swap_cells(scratch, int(round(scratch.shape[0] ** 0.5))).T
    mid_ref[...] = mid
    project(mid, w_in_ref[...], proj2_ref, sent_ref, (1, 0))


def turn(
    got_ref, mid_ref, proj_ref, grad_out_ref, w_out_ref,
    new_ref, sent_ref, grad_gate_ref, grad_w_ref, scratch,
):
    h = got_ref.shape[0] // PARTS
    n = new_ref.shape[0]
    out, normed, rstd, post = finish(summed(got_ref), w_out_ref[...])
    gate = jax.nn.sigmoid(proj_ref[4 * h :, :])
    new = (mid_ref[...] + gate * out).T
    scratch[...] = new
    new_ref[...] = swap_cells(scratch, n).reshape(new_ref.shape)
    grad_new = swap_cells(grad_out_ref, n).T
    grad, grad_gate, grad_w = finish_back(grad_new, gate, out, normed, rstd, post, w_out_ref[...])
    grad = grad.astype(BF16)
    half = sent_ref.shape[2]
    for at, channel, run in owners(sent_ref.shape[0], h):
        for k in range(2):
            sent_ref[at : at + run, k, :] = grad[channel : channel + run, k * half : (k + 1) * half]
    grad_gate_ref[...] = grad_gate
    grad_w_ref[...] = grad_w


def between(
    got_ref, mid_ref, proj2_ref, grad_gate2_ref, w_in_ref, grad_out_ref, mixed_ref, proj1_ref, w_out_ref,
    sent_ref, grad_gate_ref, grad_mid_ref, grad_wout_ref, scratch,
):
    h, _, cells = got_ref.shape
    back, low, grad_proj = project_back(
        mid_ref[...], proj2_ref, w_in_ref[...], got_ref[:, 1, :].astype(F32), got_ref[:, 0, :].astype(F32),
        grad_gate2_ref[...],
    )
    scratch[...] = back.T
    n = int(round(scratch.shape[0] ** 0.5))
    grad_mid = (grad_out_ref[...] + swap_cells(scratch, n)).T
    grad_mid_ref[...] = grad_mid
    w_out = w_out_ref[...]
    out, normed, rstd, post = finish(mixed_ref[...], w_out)
    gate = jax.nn.sigmoid(proj1_ref[4 * h :, :])
    grad, grad_gate, grad_w = finish_back(grad_mid, gate, out, normed, rstd, post, w_out)
    grad_gate_ref[...] = grad_gate
    grad_wout_ref[...] = grad_w
    grad = grad.astype(BF16)
    half = cells // 2
    count = sent_ref.shape[0]
    wide = sent_ref.shape[2] - half
    pairs = low.shape[0] // 2
    weights = [
        dot(low, grad_proj[at : at + wide], 1, 1).astype(BF16) for at in range(0, grad_proj.shape[0], wide)
    ]
    for at, channel, run in owners(count, h):
        block, first = at // pairs, at % pairs
        for k in range(2):
            rows = weights[block][k * pairs + first : k * pairs + first + run]
            sent_ref[at : at + run, k, :] = jnp.concatenate(
                [grad[channel : channel + run, k * half : (k + 1) * half], rows], axis=1
            )


def last(
    got_ref, pair_t_ref, proj_ref, grad_gate_ref, w_in_ref, grad_mid_ref, wout1_ref, wout2_ref,
    pair_grad_ref, weights_ref,
):
    back, low, grad_proj = project_back(
        pair_t_ref[...], proj_ref, w_in_ref[...], got_ref[:, 0, :].astype(F32), got_ref[:, 1, :].astype(F32),
        grad_gate_ref[...],
    )
    c = low.shape[0]
    rows = [dot(low, grad_proj[at : at + c], 1, 1) for at in range(0, grad_proj.shape[0], c)]
    weights_ref[...] = jnp.concatenate(rows + [wout1_ref[...], wout2_ref[...]], axis=0).astype(BF16)
    pair_grad_ref[...] = (grad_mid_ref[...] + back).T


def blocks(x, outer, inner, size, wide):
    rows = []
    for r in range(inner):
        rows.append(
            jnp.concatenate(
                [x[o * size : (o + 1) * size, r * wide : (r + 1) * wide] for o in range(outer)], axis=1
            )
        )
    return jnp.concatenate(rows, axis=0)


def reorder(ref, outer, inner):
    return jnp.concatenate([ref[pl.ds(r, outer, stride=inner), :] for r in range(inner)], axis=0)


def multiply(size, wide, got_ref, sent_ref, first_out_ref, second_out_ref, scratch):
    part = got_ref.shape[0] // size
    first = blocks(got_ref[:, 0, :].astype(F32), part, wide, size, wide).astype(BF16)
    scratch[...] = blocks(got_ref[:, 1, :].astype(F32), part, wide, size, wide)
    second = reorder(scratch, wide, size).astype(BF16)
    first_out_ref[...] = first
    second_out_ref[...] = second
    out = blocks(dot(first, second, 1, 1), wide, size, size, wide).astype(BF16)
    half = sent_ref.shape[2]
    sent_ref[:, 0, :] = out[:, :half]
    sent_ref[:, 1, :] = out[:, half:]


def multiply_back(size, wide, got_ref, first_ref, second_ref, *refs):
    sent_ref, scratch = refs[0], refs[-1]
    part = sent_ref.shape[0] // size
    got = [got_ref[:, k, :].astype(F32) for k in range(2)]
    half = wide * wide // 2
    if len(refs) > 2:
        sums = [jnp.sum(x[:, half:], axis=0, keepdims=True) for x in got]
        empty = jnp.zeros((refs[1].shape[0] - len(sums), sums[0].shape[1]), F32)
        refs[1][...] = jnp.concatenate(sums + [empty], axis=0).astype(BF16)
    got = jnp.concatenate([x[:, :half] for x in got], axis=1)
    grad = blocks(got, size, wide, size, wide).astype(BF16)
    sent_ref[:, 0, :] = blocks(dot(grad, second_ref[...], 1, 0), wide, part, size, wide).astype(BF16)
    scratch[...] = dot(grad, first_ref[...], 0, 0)
    sent_ref[:, 1, :] = blocks(reorder(scratch, size, wide), wide, part, size, wide).astype(BF16)


def total_of(refs):
    total = refs[0].astype(F32)
    for ref in refs[1:]:
        total += ref.astype(F32)
    return total.astype(BF16)


def sum_near(got_ref, slice_ref, sent_ref):
    rows = got_ref.shape[1]
    total = total_of([got_ref[i] for i in range(got_ref.shape[0])])
    wide = slice_ref.shape[1]
    for i in range(sent_ref.shape[0]):
        sent_ref[i, :rows, :] = total
        sent_ref[i, rows:, :wide] = slice_ref[...]
        sent_ref[i, rows:, wide:] = jnp.zeros((slice_ref.shape[0], sent_ref.shape[2] - wide), BF16)


def sum_far(got_ref, sent_ref):
    count = got_ref.shape[0]
    rows = sent_ref.shape[1] - 2 * count
    total = total_of([got_ref[i, :rows, :] for i in range(count)]).astype(F32)
    slices = [got_ref[i, rows:, :].astype(F32)[:2] for i in range(count)]
    total = jnp.concatenate([total] + slices, axis=0).astype(BF16)
    for i in range(sent_ref.shape[0]):
        sent_ref[i] = total


def unpack(scale, far, wide, got_ref, win1_ref, wout1_ref, win2_ref, wout2_ref):
    near, rows, c = got_ref.shape
    rows -= 2 * far
    flat = jnp.concatenate([got_ref[i, :rows, :] for i in range(near)], axis=0).astype(F32) * scale
    win_rows = win1_ref.shape[1]
    for at in range(0, win_rows, c):
        win1_ref[:, at : at + c] = flat[at : at + c]
    h = wout1_ref.shape[0]
    wout1_ref[...] = flat[win_rows : win_rows + h]
    wout2_ref[...] = flat[win_rows + h :]
    size = near // SPLIT
    blocks_of = win_rows // wide // SPLIT
    run = far // blocks_of
    for k in range(2):
        for r in range(run):
            pieces = []
            for a in range(SPLIT):
                for b in range(blocks_of):
                    at = rows + (b * run + r) * 2 + k
                    pieces.append(got_ref[a * size : (a + 1) * size, at, :].astype(F32)[:, :wide])
            at = (k * run + r) * size
            win2_ref[at : at + size, :] = jnp.concatenate(pieces, axis=1) * scale


def call(body, outs, *args, scratch=None):
    return pl.pallas_call(
        body,
        out_shape=[jax.ShapeDtypeStruct(s, t) for s, t in outs],
        scratch_shapes=[] if scratch is None else [pltpu.VMEM(scratch, F32)],
        compiler_params=pltpu.CompilerParams(vmem_limit_bytes=16 * 1024 * 1024),
    )(*args)


def exchange(x, axes):
    return lax.all_to_all(x, axes, 0, 0, tiled=True)


def local(pair, grad_out, w_in_out, w_out_out, w_in_in, w_out_in):
    n, _, c = pair.shape
    h = w_out_out.shape[0]
    wide = w_in_out.shape[1]
    size = lax.axis_size(ROW)
    cells = n * n
    part = size // PARTS
    low = (h, cells)
    k_shape = (size * n, part * n)
    pair = pair.reshape(cells, c)
    grad_out = grad_out.reshape(cells, c)

    cell_array = ((c, cells), F32)
    near = ((h, 2, cells), BF16)
    all_devices = ((size * size, 2, cells // 2), BF16)

    def product(sent, group, everyone):
        sent, first, second = call(
            functools.partial(multiply, size, n),
            [all_devices, (k_shape, BF16), (k_shape, BF16)],
            exchange(sent, group), scratch=k_shape,
        )
        return exchange(sent, everyone), first, second

    def product_back(sent, first, second, group, everyone, *extra):
        sent, *rest = call(
            functools.partial(multiply_back, size, n), [near, *extra],
            exchange(sent, everyone), first, second, scratch=k_shape,
        )
        return (exchange(sent, group), *rest)

    one = (("col_a", "col_b") + ROW, COL + ROW)
    two = (("row_a", "row_b") + COL, ROW + COL)
    slice_wide = wide * c // (2 * size * size)

    sent, proj1, pair_t = call(start_one, [near, ((wide, cells), F32), cell_array], pair, w_in_out)
    got, first1, second1 = product(sent, *one)
    sent, proj2, mixed1, mid_t = call(
        middle,
        [near, ((wide, cells), F32), (low, F32), cell_array],
        got, pair_t, proj1, w_out_out, w_in_in, scratch=(cells, c),
    )
    got, first2, second2 = product(sent, *two)
    pair_new, sent, grad_gate2, grad_wout_in = call(
        turn,
        [((n, n, c), F32), all_devices, cell_array, ((h, c), F32)],
        got, mid_t, proj2, grad_out, w_out_in, scratch=(cells, c),
    )
    got, = product_back(sent, first2, second2, *two)
    sent, grad_gate1, grad_mid, grad_wout_out = call(
        between,
        [((size * size, 2, cells // 2 + slice_wide), BF16), cell_array, cell_array, ((h, c), F32)],
        got, mid_t, proj2, grad_gate2, w_in_in, grad_out, mixed1, proj1, w_out_out, scratch=(cells, c),
    )
    got, win2_slice = product_back(sent, first1, second1, *one, ((8, slice_wide), BF16))
    near_count, far_count = lax.axis_size(NEAR), lax.axis_size(FAR)
    weight_rows = wide + 2 * h
    pair_grad, weights = call(
        last,
        [((cells, c), F32), ((weight_rows, c), BF16)],
        got, pair_t, proj1, grad_gate1, w_in_out, grad_mid, grad_wout_out, grad_wout_in,
    )

    each = weight_rows // near_count
    got = exchange(weights.reshape(near_count, each, c), NEAR)
    sent, = call(sum_near, [((far_count, each + 8, c), BF16)], got, win2_slice)
    sent, = call(sum_far, [((near_count, each + 2 * far_count, c), BF16)], exchange(sent, FAR))
    outs = call(
        functools.partial(unpack, 1.0 / (n * size), far_count, slice_wide),
        [((c, wide), F32), ((h, c), F32), ((c, wide), F32), ((h, c), F32)],
        exchange(sent, NEAR),
    )
    return (pair_new, pair_grad.reshape(n, n, c), *outs)


def solution(mesh):
    rows, cols = (size // (SPLIT * PARTS) for size in mesh.devices.shape)
    fine = Mesh(mesh.devices.reshape(SPLIT, PARTS, rows, SPLIT, PARTS, cols), ROW + COL)
    cell = P(ROW, COL, None)
    return jax.shard_map(
        local,
        mesh=fine,
        in_specs=(cell, cell, P(), P(), P(), P()),
        out_specs=(cell, cell, P(), P(), P(), P()),
        check_vma=False,
    )
```

```python
import functools

import jax
import jax.numpy as jnp
from jax import lax
from jax.experimental import pallas as pl
from jax.experimental.pallas import tpu as pltpu
from jax.sharding import Mesh
from jax.sharding import PartitionSpec as P

EPS = 1e-05
F32 = jnp.float32
BF16 = jnp.bfloat16
PARTS = 4
SPLIT = 2
ROW = ("row_a", "row_q", "row_b")
COL = ("col_a", "col_q", "col_b")
NEAR = ROW
FAR = COL


def dot(a, b, ca, cb):
    return lax.dot_general(a, b, (((ca,), (cb,)), ((), ())), preferred_element_type=F32)


def norm(x):
    center = x - jnp.mean(x, axis=0, keepdims=True)
    rstd = lax.rsqrt(jnp.mean(center * center, axis=0, keepdims=True) + EPS)
    return center * rstd, rstd


def norm_back(grad, normed, rstd):
    return rstd * (
        grad
        - jnp.mean(grad, axis=0, keepdims=True)
        - normed * jnp.mean(grad * normed, axis=0, keepdims=True)
    )


def swap_cells(ref, n):
    return jnp.concatenate([ref[pl.ds(j, n, stride=n), :] for j in range(n)], axis=0)


def project(normed, w_in, proj_ref, sent_ref, order):
    h = sent_ref.shape[0]
    proj = dot(w_in, normed, 0, 0)
    proj_ref[...] = proj
    for at, place in zip((0, 2 * h), order):
        gated = jax.nn.sigmoid(proj[at + h : at + 2 * h]) * proj[at : at + h]
        sent_ref[:, place, :] = gated.astype(BF16)


def project_back(x, proj_ref, w_in, gl, gr, grad_gate):
    h = gl.shape[0]
    normed, rstd = norm(x)
    sa = jax.nn.sigmoid(proj_ref[h : 2 * h, :])
    sb = jax.nn.sigmoid(proj_ref[3 * h : 4 * h, :])
    gate = jax.nn.sigmoid(proj_ref[4 * h :, :])
    gla, grb = gl * sa, gr * sb
    grad = jnp.concatenate(
        [
            gla,
            gla * proj_ref[:h, :] * (1 - sa),
            grb,
            grb * proj_ref[2 * h : 3 * h, :] * (1 - sb),
            grad_gate * gate * (1 - gate),
        ],
        axis=0,
    ).astype(BF16)
    return norm_back(dot(w_in, grad, 1, 0), normed, rstd), normed.astype(BF16), grad


def finish(mixed, w_out):
    normed, rstd = norm(mixed)
    post = normed.astype(BF16)
    return dot(w_out, post, 0, 0), normed, rstd, post


def finish_back(grad_new, gate, out, normed, rstd, post, w_out):
    grad_gate = grad_new * out
    grad_proj = (grad_new * gate).astype(BF16)
    grad_w = dot(post, grad_proj, 1, 1)
    return norm_back(dot(w_out, grad_proj, 1, 0), normed, rstd), grad_gate, grad_w


def owners(count, h):
    run = h // SPLIT
    return [(at, (at // run // PARTS) * run, run) for at in range(0, count, run)]


def summed(got_ref):
    count = got_ref.shape[0]
    h = count // PARTS

    def total(k):
        sums = {}
        for at, channel, run in owners(count, h):
            part = got_ref[at : at + run, k, :].astype(F32)
            sums[channel] = sums[channel] + part if channel in sums else part
        return jnp.concatenate(list(sums.values()), axis=0)

    return jnp.concatenate([total(0), total(1)], axis=1)


def turn_pair(pair_ref, pair_t_ref, normed_ref):
    x = pair_ref[...].T
    pair_t_ref[...] = x
    normed_ref[...] = norm(x)[0].astype(BF16)


def start_one(normed_ref, w_ref, sent_ref, proj_ref):
    project(normed_ref[...], w_ref[...], proj_ref, sent_ref, (0, 1))


def middle(
    got_ref, pair_t_ref, proj1_ref, w_out_ref, w_in_ref,
    sent_ref, proj2_ref, mixed_ref, mid_ref, scratch,
):
    h = sent_ref.shape[0]
    mixed = summed(got_ref)
    mixed_ref[...] = mixed
    out, *_ = finish(mixed, w_out_ref[...])
    mid = pair_t_ref[...] + jax.nn.sigmoid(proj1_ref[4 * h :, :]) * out
    scratch[...] = mid.T
    mid = swap_cells(scratch, int(round(scratch.shape[0] ** 0.5))).T
    mid_ref[...] = mid
    project(norm(mid)[0].astype(BF16), w_in_ref[...], proj2_ref, sent_ref, (1, 0))


def turn(
    got_ref, mid_ref, proj_ref, grad_out_ref, w_out_ref,
    new_ref, sent_ref, grad_gate_ref, grad_w_ref, scratch,
):
    h = got_ref.shape[0] // PARTS
    n = new_ref.shape[0]
    out, normed, rstd, post = finish(summed(got_ref), w_out_ref[...])
    gate = jax.nn.sigmoid(proj_ref[4 * h :, :])
    new = (mid_ref[...] + gate * out).T
    scratch[...] = new
    new_ref[...] = swap_cells(scratch, n).reshape(new_ref.shape)
    grad_new = swap_cells(grad_out_ref, n).T
    grad, grad_gate, grad_w = finish_back(grad_new, gate, out, normed, rstd, post, w_out_ref[...])
    grad = grad.astype(BF16)
    half = sent_ref.shape[2]
    for at, channel, run in owners(sent_ref.shape[0], h):
        for k in range(2):
            sent_ref[at : at + run, k, :] = grad[channel : channel + run, k * half : (k + 1) * half]
    grad_gate_ref[...] = grad_gate
    grad_w_ref[...] = grad_w


def between(
    got_ref, mid_ref, proj2_ref, grad_gate2_ref, w_in_ref, grad_out_ref, mixed_ref, proj1_ref, w_out_ref,
    sent_ref, grad_gate_ref, grad_mid_ref, grad_wout_ref, scratch,
):
    h, _, cells = got_ref.shape
    back, low, grad_proj = project_back(
        mid_ref[...], proj2_ref, w_in_ref[...], got_ref[:, 1, :].astype(F32), got_ref[:, 0, :].astype(F32),
        grad_gate2_ref[...],
    )
    scratch[...] = back.T
    n = int(round(scratch.shape[0] ** 0.5))
    grad_mid = (grad_out_ref[...] + swap_cells(scratch, n)).T
    grad_mid_ref[...] = grad_mid
    w_out = w_out_ref[...]
    out, normed, rstd, post = finish(mixed_ref[...], w_out)
    gate = jax.nn.sigmoid(proj1_ref[4 * h :, :])
    grad, grad_gate, grad_w = finish_back(grad_mid, gate, out, normed, rstd, post, w_out)
    grad_gate_ref[...] = grad_gate
    grad_wout_ref[...] = grad_w
    grad = grad.astype(BF16)
    half = cells // 2
    count = sent_ref.shape[0]
    wide = sent_ref.shape[2] - half
    pairs = low.shape[0] // 2
    weights = [
        dot(low, grad_proj[at : at + wide], 1, 1).astype(BF16) for at in range(0, grad_proj.shape[0], wide)
    ]
    for at, channel, run in owners(count, h):
        block, first = at // pairs, at % pairs
        for k in range(2):
            rows = weights[block][k * pairs + first : k * pairs + first + run]
            sent_ref[at : at + run, k, :] = jnp.concatenate(
                [grad[channel : channel + run, k * half : (k + 1) * half], rows], axis=1
            )


def last(
    got_ref, pair_t_ref, proj_ref, grad_gate_ref, w_in_ref, grad_mid_ref, wout1_ref, wout2_ref,
    pair_grad_ref, weights_ref,
):
    back, low, grad_proj = project_back(
        pair_t_ref[...], proj_ref, w_in_ref[...], got_ref[:, 0, :].astype(F32), got_ref[:, 1, :].astype(F32),
        grad_gate_ref[...],
    )
    c = low.shape[0]
    rows = [dot(low, grad_proj[at : at + c], 1, 1) for at in range(0, grad_proj.shape[0], c)]
    weights_ref[...] = jnp.concatenate(rows + [wout1_ref[...], wout2_ref[...]], axis=0).astype(BF16)
    pair_grad_ref[...] = (grad_mid_ref[...] + back).T


def blocks(x, outer, inner, size, wide):
    rows = []
    for r in range(inner):
        rows.append(
            jnp.concatenate(
                [x[o * size : (o + 1) * size, r * wide : (r + 1) * wide] for o in range(outer)], axis=1
            )
        )
    return jnp.concatenate(rows, axis=0)


def blocks_low(x, outer, inner, size, wide):
    lanes = 128
    width = -(-wide * (outer + inner) // lanes) * lanes
    lane = lax.broadcasted_iota(jnp.int32, (size, lanes), 1)

    def masks(diagonal):
        low, high = diagonal * wide, (diagonal + 1) * wide
        return [
            (t, (lane >= low - t * lanes) & (lane < high - t * lanes))
            for t in range(low // lanes, (high - 1) // lanes + 1)
        ]

    chosen = [masks(diagonal) for diagonal in range(outer + inner - 1)]
    empty = jnp.zeros((size, width - inner * wide), x.dtype)
    turned = []
    for o in range(outer):
        row = jnp.concatenate([x[o * size : (o + 1) * size], empty], axis=1)
        turned.append(pltpu.roll(row, o * wide, 1) if o else row)
    rows = []
    for r in range(inner):
        merged = [None] * (width // lanes)
        for o in range(outer):
            for t, mask in chosen[r + o]:
                piece = turned[o][:, t * lanes : (t + 1) * lanes]
                merged[t] = piece if merged[t] is None else jnp.where(mask, piece, merged[t])
        zero = jnp.zeros((size, lanes), x.dtype)
        row = jnp.concatenate([zero if m is None else m for m in merged], axis=1)
        row = pltpu.roll(row, width - r * wide, 1) if r else row
        rows.append(row[:, : outer * wide])
    return jnp.concatenate(rows, axis=0)


def reorder(ref, outer, inner):
    return jnp.concatenate([ref[pl.ds(r, outer, stride=inner), :] for r in range(inner)], axis=0)


def multiply(size, wide, got_ref, sent_ref, first_out_ref, second_out_ref, scratch):
    part = got_ref.shape[0] // size
    first = blocks_low(got_ref[:, 0, :], part, wide, size, wide)
    scratch[...] = blocks_low(got_ref[:, 1, :], part, wide, size, wide).astype(F32)
    second = reorder(scratch, wide, size).astype(BF16)
    first_out_ref[...] = first
    second_out_ref[...] = second
    out = blocks_low(dot(first, second, 1, 1).astype(BF16), wide, size, size, wide)
    half = sent_ref.shape[2]
    sent_ref[:, 0, :] = out[:, :half]
    sent_ref[:, 1, :] = out[:, half:]


def multiply_back(size, wide, got_ref, first_ref, second_ref, *refs):
    sent_ref, scratch = refs[0], refs[-1]
    part = sent_ref.shape[0] // size
    got = [got_ref[:, k, :].astype(F32) for k in range(2)]
    half = wide * wide // 2
    if len(refs) > 2:
        sums = [jnp.sum(x[:, half:], axis=0, keepdims=True) for x in got]
        empty = jnp.zeros((refs[1].shape[0] - len(sums), sums[0].shape[1]), F32)
        refs[1][...] = jnp.concatenate(sums + [empty], axis=0).astype(BF16)
    got = jnp.concatenate([x[:, :half] for x in got], axis=1)
    grad = blocks(got, size, wide, size, wide).astype(BF16)
    sent_ref[:, 0, :] = blocks(dot(grad, second_ref[...], 1, 0), wide, part, size, wide).astype(BF16)
    scratch[...] = dot(grad, first_ref[...], 0, 0)
    sent_ref[:, 1, :] = blocks(reorder(scratch, size, wide), wide, part, size, wide).astype(BF16)


def total_of(refs):
    total = refs[0].astype(F32)
    for ref in refs[1:]:
        total += ref.astype(F32)
    return total.astype(BF16)


def sum_near(got_ref, slice_ref, sent_ref):
    rows = got_ref.shape[1]
    total = total_of([got_ref[i] for i in range(got_ref.shape[0])])
    wide = slice_ref.shape[1]
    for i in range(sent_ref.shape[0]):
        sent_ref[i, :rows, :] = total
        sent_ref[i, rows:, :wide] = slice_ref[...]
        sent_ref[i, rows:, wide:] = jnp.zeros((slice_ref.shape[0], sent_ref.shape[2] - wide), BF16)


def sum_far(got_ref, sent_ref):
    count = got_ref.shape[0]
    rows = sent_ref.shape[1] - 2 * count
    total = total_of([got_ref[i, :rows, :] for i in range(count)]).astype(F32)
    slices = [got_ref[i, rows:, :].astype(F32)[:2] for i in range(count)]
    total = jnp.concatenate([total] + slices, axis=0).astype(BF16)
    for i in range(sent_ref.shape[0]):
        sent_ref[i] = total


def unpack(scale, far, wide, got_ref, win1_ref, wout1_ref, win2_ref, wout2_ref, scratch):
    near, rows, c = got_ref.shape
    rows -= 2 * far
    scratch[...] = got_ref[:, rows:, :].reshape(scratch.shape).astype(F32)
    flat = jnp.concatenate([got_ref[i, :rows, :] for i in range(near)], axis=0).astype(F32) * scale
    win_rows = win1_ref.shape[1]
    for at in range(0, win_rows, c):
        win1_ref[:, at : at + c] = flat[at : at + c]
    h = wout1_ref.shape[0]
    wout1_ref[...] = flat[win_rows : win_rows + h]
    wout2_ref[...] = flat[win_rows + h :]
    run = far // (win_rows // wide)
    for k in range(2):
        for r in range(run):
            pieces = [
                scratch[pl.ds((at + r) * 2 + k, near, stride=2 * far), :][:, :wide] for at in range(0, far, run)
            ]
            at = (k * run + r) * near
            win2_ref[at : at + near, :] = jnp.concatenate(pieces, axis=1) * scale


def call(body, outs, *args, scratch=None):
    return pl.pallas_call(
        body,
        out_shape=[jax.ShapeDtypeStruct(s, t) for s, t in outs],
        scratch_shapes=[] if scratch is None else [pltpu.VMEM(scratch, F32)],
        compiler_params=pltpu.CompilerParams(vmem_limit_bytes=16 * 1024 * 1024),
    )(*args)


def exchange(x, axes):
    return lax.all_to_all(x, axes, 0, 0, tiled=True)


def local(pair, grad_out, w_in_out, w_out_out, w_in_in, w_out_in):
    n, _, c = pair.shape
    h = w_out_out.shape[0]
    wide = w_in_out.shape[1]
    size = lax.axis_size(ROW)
    cells = n * n
    part = size // PARTS
    low = (h, cells)
    k_shape = (size * n, part * n)
    pair = pair.reshape(cells, c)
    grad_out = grad_out.reshape(cells, c)

    cell_array = ((c, cells), F32)
    near = ((h, 2, cells), BF16)
    all_devices = ((size * size, 2, cells // 2), BF16)

    def product(sent, group, everyone):
        sent, first, second = call(
            functools.partial(multiply, size, n),
            [all_devices, (k_shape, BF16), (k_shape, BF16)],
            exchange(sent, group), scratch=k_shape,
        )
        return exchange(sent, everyone), first, second

    def product_back(sent, first, second, group, everyone, *extra):
        sent, *rest = call(
            functools.partial(multiply_back, size, n), [near, *extra],
            exchange(sent, everyone), first, second, scratch=k_shape,
        )
        return (exchange(sent, group), *rest)

    one = (("col_a", "col_b") + ROW, COL + ROW)
    two = (("row_a", "row_b") + COL, ROW + COL)
    slice_wide = wide * c // (2 * size * size)

    pair_t, normed1 = call(turn_pair, [cell_array, ((c, cells), BF16)], pair)
    sent, proj1 = call(start_one, [near, ((wide, cells), F32)], normed1, w_in_out)
    got, first1, second1 = product(sent, *one)
    sent, proj2, mixed1, mid_t = call(
        middle,
        [near, ((wide, cells), F32), (low, F32), cell_array],
        got, pair_t, proj1, w_out_out, w_in_in, scratch=(cells, c),
    )
    got, first2, second2 = product(sent, *two)
    pair_new, sent, grad_gate2, grad_wout_in = call(
        turn,
        [((n, n, c), F32), all_devices, cell_array, ((h, c), F32)],
        got, mid_t, proj2, grad_out, w_out_in, scratch=(cells, c),
    )
    got, = product_back(sent, first2, second2, *two)
    sent, grad_gate1, grad_mid, grad_wout_out = call(
        between,
        [((size * size, 2, cells // 2 + slice_wide), BF16), cell_array, cell_array, ((h, c), F32)],
        got, mid_t, proj2, grad_gate2, w_in_in, grad_out, mixed1, proj1, w_out_out, scratch=(cells, c),
    )
    got, win2_slice = product_back(sent, first1, second1, *one, ((8, slice_wide), BF16))
    near_count, far_count = lax.axis_size(NEAR), lax.axis_size(FAR)
    weight_rows = wide + 2 * h
    pair_grad, weights = call(
        last,
        [((cells, c), F32), ((weight_rows, c), BF16)],
        got, pair_t, proj1, grad_gate1, w_in_out, grad_mid, grad_wout_out, grad_wout_in,
    )

    each = weight_rows // near_count
    got = exchange(weights.reshape(near_count, each, c), NEAR)
    sent, = call(sum_near, [((far_count, each + 8, c), BF16)], got, win2_slice)
    sent, = call(sum_far, [((near_count, each + 2 * far_count, c), BF16)], exchange(sent, FAR))
    outs = call(
        functools.partial(unpack, 1.0 / (n * size), far_count, slice_wide),
        [((c, wide), F32), ((h, c), F32), ((c, wide), F32), ((h, c), F32)],
        exchange(sent, NEAR), scratch=(near_count * 2 * far_count, c),
    )
    return (pair_new, pair_grad.reshape(n, n, c), *outs)


def solution(mesh):
    rows, cols = (size // (SPLIT * PARTS) for size in mesh.devices.shape)
    fine = Mesh(mesh.devices.reshape(SPLIT, PARTS, rows, SPLIT, PARTS, cols), ROW + COL)
    cell = P(ROW, COL, None)
    return jax.shard_map(
        local,
        mesh=fine,
        in_specs=(cell, cell, P(), P(), P(), P()),
        out_specs=(cell, cell, P(), P(), P(), P()),
        check_vma=False,
    )
```

```python
import functools

import jax
import jax.numpy as jnp
from jax import lax
from jax.experimental import pallas as pl
from jax.experimental.pallas import tpu as pltpu
from jax.sharding import Mesh
from jax.sharding import PartitionSpec as P

EPS = 1e-05
F32 = jnp.float32
BF16 = jnp.bfloat16
TILE = 128
PAIRS = (1536, TILE)
PARTS = 4
SPLIT = 2
ROW = ("row_a", "row_q", "row_b")
COL = ("col_a", "col_q", "col_b")
NEAR = ROW
FAR = COL


def dot(a, b, ca, cb):
    return lax.dot_general(a, b, (((ca,), (cb,)), ((), ())), preferred_element_type=F32)


def norm(x):
    center = x - jnp.mean(x, axis=0, keepdims=True)
    rstd = lax.rsqrt(jnp.mean(center * center, axis=0, keepdims=True) + EPS)
    return center * rstd, rstd


def norm_back(grad, normed, rstd):
    return rstd * (
        grad
        - jnp.mean(grad, axis=0, keepdims=True)
        - normed * jnp.mean(grad * normed, axis=0, keepdims=True)
    )


def read_pairs(ref, scratch):
    count, _, lanes = ref.shape
    rows = [], []
    for tile in range(-(-lanes // TILE)):
        low, high = tile * TILE, min(lanes, (tile + 1) * TILE)
        x = ref[:, :, low:high]
        if high - low < TILE:
            x = jnp.concatenate([x, jnp.zeros((count, 2, TILE - (high - low)), x.dtype)], axis=2)
        at = tile * 2 * count
        scratch[at : at + 2 * count, :] = x.reshape(2 * count, TILE).astype(F32)
        for k in range(2):
            rows[k].append(scratch[pl.ds(at + k, count, stride=2), :][:, : high - low])
    return [jnp.concatenate(x, axis=1) for x in rows]


def write_pairs(ref, pair, scratch):
    count, _, lanes = ref.shape
    for tile in range(-(-lanes // TILE)):
        low, high = tile * TILE, min(lanes, (tile + 1) * TILE)
        at = tile * 2 * count
        for k in range(2):
            x = pair[k][:, low:high]
            if high - low < TILE:
                x = jnp.concatenate([x, jnp.zeros((count, TILE - (high - low)), F32)], axis=1)
            scratch[pl.ds(at + k, count, stride=2), :] = x
        x = scratch[at : at + 2 * count, :].astype(BF16).reshape(count, 2, TILE)
        ref[:, :, low:high] = x[:, :, : high - low]


def write_plain(ref, pair):
    for k in range(2):
        ref[:, k, :] = pair[k].astype(BF16)


def swap_cells(ref, n):
    return jnp.concatenate([ref[pl.ds(j, n, stride=n), :] for j in range(n)], axis=0)


def project(normed, w_in, proj_ref, sent_ref, order, pairs_out):
    h = sent_ref.shape[0]
    proj = dot(w_in, normed, 0, 0)
    proj_ref[...] = proj
    gated = [jax.nn.sigmoid(proj[at + h : at + 2 * h]) * proj[at : at + h] for at in (0, 2 * h)]
    write_plain(sent_ref, [gated[place] for place in order])


def project_back(x, proj_ref, w_in, gl, gr, grad_gate):
    h = gl.shape[0]
    normed, rstd = norm(x)
    sa = jax.nn.sigmoid(proj_ref[h : 2 * h, :])
    sb = jax.nn.sigmoid(proj_ref[3 * h : 4 * h, :])
    gate = jax.nn.sigmoid(proj_ref[4 * h :, :])
    gla, grb = gl * sa, gr * sb
    grad = jnp.concatenate(
        [
            gla,
            gla * proj_ref[:h, :] * (1 - sa),
            grb,
            grb * proj_ref[2 * h : 3 * h, :] * (1 - sb),
            grad_gate * gate * (1 - gate),
        ],
        axis=0,
    ).astype(BF16)
    return norm_back(dot(w_in, grad, 1, 0), normed, rstd), normed.astype(BF16), grad


def finish(mixed, w_out):
    normed, rstd = norm(mixed)
    post = normed.astype(BF16)
    return dot(w_out, post, 0, 0), normed, rstd, post


def finish_back(grad_new, gate, out, normed, rstd, post, w_out):
    grad_gate = grad_new * out
    grad_proj = (grad_new * gate).astype(BF16)
    grad_w = dot(post, grad_proj, 1, 1)
    return norm_back(dot(w_out, grad_proj, 1, 0), normed, rstd), grad_gate, grad_w


def owners(count, h):
    run = h // SPLIT
    return [(at, (at // run // PARTS) * run, run) for at in range(0, count, run)]


def summed(got_ref):
    count = got_ref.shape[0]
    h = count // PARTS
    def total(k):
        sums = {}
        for at, channel, run in owners(count, h):
            part = got_ref[at : at + run, k, :].astype(F32)
            sums[channel] = sums[channel] + part if channel in sums else part
        return jnp.concatenate(list(sums.values()), axis=0)

    return jnp.concatenate([total(0), total(1)], axis=1)


def to_owners(x):
    h, cells = x.shape
    runs = [x[channel : channel + run] for _, channel, run in owners(PARTS * h, h)]
    x = jnp.concatenate(runs, axis=0)
    return [x[:, : cells // 2], x[:, cells // 2 :]]


def turn_pair(pair_ref, pair_t_ref, normed_ref):
    x = pair_ref[...].T
    pair_t_ref[...] = x
    normed_ref[...] = norm(x)[0].astype(BF16)


def start_one(normed_ref, w_ref, sent_ref, proj_ref, pairs_out):
    project(normed_ref[...], w_ref[...], proj_ref, sent_ref, (0, 1), pairs_out)


def middle(
    got_ref, pair_t_ref, proj1_ref, w_out_ref, w_in_ref,
    sent_ref, proj2_ref, mixed_ref, mid_ref, scratch, pairs_out,
):
    h = sent_ref.shape[0]
    mixed = summed(got_ref)
    mixed_ref[...] = mixed
    out, *_ = finish(mixed, w_out_ref[...])
    mid = pair_t_ref[...] + jax.nn.sigmoid(proj1_ref[4 * h :, :]) * out
    scratch[...] = mid.T
    mid = swap_cells(scratch, int(round(scratch.shape[0] ** 0.5))).T
    mid_ref[...] = mid
    project(norm(mid)[0].astype(BF16), w_in_ref[...], proj2_ref, sent_ref, (1, 0), pairs_out)


def turn(
    got_ref, mid_ref, proj_ref, grad_out_ref, w_out_ref,
    new_ref, sent_ref, grad_gate_ref, grad_w_ref, scratch, pairs_out,
):
    h = got_ref.shape[0] // PARTS
    n = new_ref.shape[0]
    out, normed, rstd, post = finish(summed(got_ref), w_out_ref[...])
    gate = jax.nn.sigmoid(proj_ref[4 * h :, :])
    new = (mid_ref[...] + gate * out).T
    scratch[...] = new
    new_ref[...] = swap_cells(scratch, n).reshape(new_ref.shape)
    grad_new = swap_cells(grad_out_ref, n).T
    grad, grad_gate, grad_w = finish_back(grad_new, gate, out, normed, rstd, post, w_out_ref[...])
    write_plain(sent_ref, to_owners(grad))
    grad_gate_ref[...] = grad_gate
    grad_w_ref[...] = grad_w


def between(
    got_ref, mid_ref, proj2_ref, grad_gate2_ref, w_in_ref, grad_out_ref, mixed_ref, proj1_ref, w_out_ref,
    sent_ref, grad_gate_ref, grad_mid_ref, grad_wout_ref, scratch, pairs_out,
):
    h, _, cells = got_ref.shape
    grad_right, grad_left = (got_ref[:, k, :].astype(F32) for k in range(2))
    back, low, grad_proj = project_back(
        mid_ref[...], proj2_ref, w_in_ref[...], grad_left, grad_right, grad_gate2_ref[...]
    )
    scratch[...] = back.T
    n = int(round(scratch.shape[0] ** 0.5))
    grad_mid = (grad_out_ref[...] + swap_cells(scratch, n)).T
    grad_mid_ref[...] = grad_mid
    w_out = w_out_ref[...]
    out, normed, rstd, post = finish(mixed_ref[...], w_out)
    gate = jax.nn.sigmoid(proj1_ref[4 * h :, :])
    grad, grad_gate, grad_w = finish_back(grad_mid, gate, out, normed, rstd, post, w_out)
    grad_gate_ref[...] = grad_gate
    grad_wout_ref[...] = grad_w
    wide = sent_ref.shape[2] - cells // 2
    pairs = low.shape[0] // 2
    weights = [dot(low, grad_proj[at : at + wide], 1, 1) for at in range(0, grad_proj.shape[0], wide)]
    sent = [
        jnp.concatenate(
            [x, jnp.concatenate([w[k * pairs : (k + 1) * pairs] for w in weights], axis=0)], axis=1
        )
        for k, x in enumerate(to_owners(grad))
    ]
    write_plain(sent_ref, sent)


def last(
    got_ref, pair_t_ref, proj_ref, grad_gate_ref, w_in_ref, grad_mid_ref, wout1_ref, wout2_ref,
    pair_grad_ref, weights_ref,
):
    grad_left, grad_right = (got_ref[:, k, :].astype(F32) for k in range(2))
    back, low, grad_proj = project_back(
        pair_t_ref[...], proj_ref, w_in_ref[...], grad_left, grad_right, grad_gate_ref[...]
    )
    c = low.shape[0]
    rows = [dot(low, grad_proj[at : at + c], 1, 1) for at in range(0, grad_proj.shape[0], c)]
    weights_ref[...] = jnp.concatenate(rows + [wout1_ref[...], wout2_ref[...]], axis=0).astype(BF16)
    pair_grad_ref[...] = (grad_mid_ref[...] + back).T


def blocks(x, outer, inner, size, wide):
    rows = []
    for r in range(inner):
        rows.append(
            jnp.concatenate(
                [x[o * size : (o + 1) * size, r * wide : (r + 1) * wide] for o in range(outer)], axis=1
            )
        )
    return jnp.concatenate(rows, axis=0)


def blocks_low(x, outer, inner, size, wide):
    lanes = 128
    width = -(-wide * (outer + inner) // lanes) * lanes
    lane = lax.broadcasted_iota(jnp.int32, (size, lanes), 1)

    def masks(diagonal):
        low, high = diagonal * wide, (diagonal + 1) * wide
        return [
            (t, (lane >= low - t * lanes) & (lane < high - t * lanes))
            for t in range(low // lanes, (high - 1) // lanes + 1)
        ]

    chosen = [masks(diagonal) for diagonal in range(outer + inner - 1)]
    empty = jnp.zeros((size, width - inner * wide), x.dtype)
    turned = []
    for o in range(outer):
        row = jnp.concatenate([x[o * size : (o + 1) * size], empty], axis=1)
        turned.append(pltpu.roll(row, o * wide, 1) if o else row)
    rows = []
    for r in range(inner):
        merged = [None] * (width // lanes)
        for o in range(outer):
            for t, mask in chosen[r + o]:
                piece = turned[o][:, t * lanes : (t + 1) * lanes]
                merged[t] = piece if merged[t] is None else jnp.where(mask, piece, merged[t])
        zero = jnp.zeros((size, lanes), x.dtype)
        row = jnp.concatenate([zero if m is None else m for m in merged], axis=1)
        row = pltpu.roll(row, width - r * wide, 1) if r else row
        rows.append(row[:, : outer * wide])
    return jnp.concatenate(rows, axis=0)


def reorder(ref, outer, inner):
    return jnp.concatenate([ref[pl.ds(r, outer, stride=inner), :] for r in range(inner)], axis=0)


def multiply(size, wide, got_ref, sent_ref, first_out_ref, second_out_ref, scratch, pairs_in, pairs_out):
    part = got_ref.shape[0] // size
    first, second = read_pairs(got_ref, pairs_in)
    first = blocks_low(first.astype(BF16), part, wide, size, wide).astype(BF16)
    scratch[...] = blocks_low(second.astype(BF16), part, wide, size, wide).astype(F32)
    second = reorder(scratch, wide, size).astype(BF16)
    first_out_ref[...] = first
    second_out_ref[...] = second
    out = blocks_low(dot(first, second, 1, 1).astype(BF16), wide, size, size, wide).astype(F32)
    half = sent_ref.shape[2]
    write_pairs(sent_ref, [out[:, :half], out[:, half:]], pairs_out)


def multiply_back(size, wide, got_ref, first_ref, second_ref, *refs):
    sent_ref, (scratch, pairs_out) = refs[0], refs[-2:]
    part = sent_ref.shape[0] // size
    got = [got_ref[:, k, :].astype(F32) for k in range(2)]
    half = wide * wide // 2
    if len(refs) > 3:
        sums = [jnp.sum(x[:, half:], axis=0, keepdims=True) for x in got]
        empty = jnp.zeros((refs[1].shape[0] - len(sums), sums[0].shape[1]), F32)
        refs[1][...] = jnp.concatenate(sums + [empty], axis=0).astype(BF16)
    got = jnp.concatenate([x[:, :half] for x in got], axis=1)
    grad = blocks(got, size, wide, size, wide).astype(BF16)
    sent = [blocks(dot(grad, second_ref[...], 1, 0), wide, part, size, wide)]
    scratch[...] = dot(grad, first_ref[...], 0, 0)
    sent.append(blocks(reorder(scratch, size, wide), wide, part, size, wide))
    write_plain(sent_ref, sent)


def total_of(refs):
    total = refs[0].astype(F32)
    for ref in refs[1:]:
        total += ref.astype(F32)
    return total.astype(BF16)


def sum_near(got_ref, slice_ref, sent_ref):
    rows = got_ref.shape[1]
    total = total_of([got_ref[i] for i in range(got_ref.shape[0])])
    wide = slice_ref.shape[1]
    for i in range(sent_ref.shape[0]):
        sent_ref[i, :rows, :] = total
        sent_ref[i, rows:, :wide] = slice_ref[...]
        sent_ref[i, rows:, wide:] = jnp.zeros((slice_ref.shape[0], sent_ref.shape[2] - wide), BF16)


def sum_far(got_ref, sent_ref):
    count = got_ref.shape[0]
    rows = sent_ref.shape[1] - 2 * count
    total = total_of([got_ref[i, :rows, :] for i in range(count)]).astype(F32)
    slices = [got_ref[i, rows:, :].astype(F32)[:2] for i in range(count)]
    total = jnp.concatenate([total] + slices, axis=0).astype(BF16)
    for i in range(sent_ref.shape[0]):
        sent_ref[i] = total


def unpack(scale, far, wide, got_ref, win1_ref, wout1_ref, win2_ref, wout2_ref, scratch):
    near, rows, c = got_ref.shape
    rows -= 2 * far
    scratch[...] = got_ref[:, rows:, :].reshape(scratch.shape).astype(F32)
    flat = jnp.concatenate([got_ref[i, :rows, :] for i in range(near)], axis=0).astype(F32) * scale
    win_rows = win1_ref.shape[1]
    for at in range(0, win_rows, c):
        win1_ref[:, at : at + c] = flat[at : at + c]
    h = wout1_ref.shape[0]
    wout1_ref[...] = flat[win_rows : win_rows + h]
    wout2_ref[...] = flat[win_rows + h :]
    run = far // (win_rows // wide)
    for k in range(2):
        for r in range(run):
            pieces = [
                scratch[pl.ds((at + r) * 2 + k, near, stride=2 * far), :][:, :wide] for at in range(0, far, run)
            ]
            at = (k * run + r) * near
            win2_ref[at : at + near, :] = jnp.concatenate(pieces, axis=1) * scale


def call(body, outs, *args, scratch=()):
    return pl.pallas_call(
        body,
        out_shape=[jax.ShapeDtypeStruct(s, t) for s, t in outs],
        scratch_shapes=[pltpu.VMEM(shape, F32) for shape in scratch],
        compiler_params=pltpu.CompilerParams(vmem_limit_bytes=16 * 1024 * 1024),
    )(*args)


def exchange(x, axes):
    return lax.all_to_all(x, axes, 0, 0, tiled=True)


def local(pair, grad_out, w_in_out, w_out_out, w_in_in, w_out_in):
    n, _, c = pair.shape
    h = w_out_out.shape[0]
    wide = w_in_out.shape[1]
    size = lax.axis_size(ROW)
    cells = n * n
    part = size // PARTS
    low = (h, cells)
    k_shape = (size * n, part * n)
    pair = pair.reshape(cells, c)
    grad_out = grad_out.reshape(cells, c)

    cell_array = ((c, cells), F32)
    near = ((h, 2, cells), BF16)
    all_devices = ((size * size, 2, cells // 2), BF16)

    def product(sent, group, everyone):
        sent, first, second = call(
            functools.partial(multiply, size, n),
            [all_devices, (k_shape, BF16), (k_shape, BF16)],
            exchange(sent, group), scratch=[k_shape, PAIRS, PAIRS],
        )
        return exchange(sent, everyone), first, second

    def product_back(sent, first, second, group, everyone, *extra):
        sent, *rest = call(
            functools.partial(multiply_back, size, n), [near, *extra],
            exchange(sent, everyone), first, second, scratch=[k_shape, PAIRS],
        )
        return (exchange(sent, group), *rest)

    one = (("col_a", "col_b") + ROW, COL + ROW)
    two = (("row_a", "row_b") + COL, ROW + COL)
    slice_wide = wide * c // (2 * size * size)

    pair_t, normed1 = call(turn_pair, [cell_array, ((c, cells), BF16)], pair)
    sent, proj1 = call(start_one, [near, ((wide, cells), F32)], normed1, w_in_out, scratch=[PAIRS])
    got, first1, second1 = product(sent, *one)
    sent, proj2, mixed1, mid_t = call(
        middle,
        [near, ((wide, cells), F32), (low, F32), cell_array],
        got, pair_t, proj1, w_out_out, w_in_in, scratch=[(cells, c), PAIRS],
    )
    got, first2, second2 = product(sent, *two)
    pair_new, sent, grad_gate2, grad_wout_in = call(
        turn,
        [((n, n, c), F32), all_devices, cell_array, ((h, c), F32)],
        got, mid_t, proj2, grad_out, w_out_in, scratch=[(cells, c), PAIRS],
    )
    got, = product_back(sent, first2, second2, *two)
    sent, grad_gate1, grad_mid, grad_wout_out = call(
        between,
        [((size * size, 2, cells // 2 + slice_wide), BF16), cell_array, cell_array, ((h, c), F32)],
        got, mid_t, proj2, grad_gate2, w_in_in, grad_out, mixed1, proj1, w_out_out, scratch=[(cells, c), PAIRS],
    )
    got, win2_slice = product_back(sent, first1, second1, *one, ((8, slice_wide), BF16))
    near_count, far_count = lax.axis_size(NEAR), lax.axis_size(FAR)
    weight_rows = wide + 2 * h
    pair_grad, weights = call(
        last,
        [((cells, c), F32), ((weight_rows, c), BF16)],
        got, pair_t, proj1, grad_gate1, w_in_out, grad_mid, grad_wout_out, grad_wout_in,
    )

    each = weight_rows // near_count
    got = exchange(weights.reshape(near_count, each, c), NEAR)
    sent, = call(sum_near, [((far_count, each + 8, c), BF16)], got, win2_slice)
    sent, = call(sum_far, [((near_count, each + 2 * far_count, c), BF16)], exchange(sent, FAR))
    outs = call(
        functools.partial(unpack, 1.0 / (n * size), far_count, slice_wide),
        [((c, wide), F32), ((h, c), F32), ((c, wide), F32), ((h, c), F32)],
        exchange(sent, NEAR), scratch=[(near_count * 2 * far_count, c)],
    )
    return (pair_new, pair_grad.reshape(n, n, c), *outs)


def solution(mesh):
    rows, cols = (size // (SPLIT * PARTS) for size in mesh.devices.shape)
    fine = Mesh(mesh.devices.reshape(SPLIT, PARTS, rows, SPLIT, PARTS, cols), ROW + COL)
    cell = P(ROW, COL, None)
    return jax.shard_map(
        local,
        mesh=fine,
        in_specs=(cell, cell, P(), P(), P(), P()),
        out_specs=(cell, cell, P(), P(), P(), P()),
        check_vma=False,
    )
```

```python
import functools

import jax
import jax.numpy as jnp
from jax import lax
from jax.experimental import pallas as pl
from jax.experimental.pallas import tpu as pltpu
from jax.sharding import Mesh
from jax.sharding import PartitionSpec as P

EPS = 1e-05
F32 = jnp.float32
BF16 = jnp.bfloat16
TILE = 128
PAIRS = (1536, TILE)
PARTS = 4
SPLIT = 2
ROW = ("row_a", "row_q", "row_b")
COL = ("col_a", "col_q", "col_b")
NEAR = ROW
FAR = COL


def dot(a, b, ca, cb):
    return lax.dot_general(a, b, (((ca,), (cb,)), ((), ())), preferred_element_type=F32)


def norm(x):
    center = x - jnp.mean(x, axis=0, keepdims=True)
    rstd = lax.rsqrt(jnp.mean(center * center, axis=0, keepdims=True) + EPS)
    return center * rstd, rstd


def norm_back(grad, normed, rstd):
    return rstd * (
        grad
        - jnp.mean(grad, axis=0, keepdims=True)
        - normed * jnp.mean(grad * normed, axis=0, keepdims=True)
    )


def read_pairs(ref, scratch):
    count, _, lanes = ref.shape
    rows = [], []
    for tile in range(-(-lanes // TILE)):
        low, high = tile * TILE, min(lanes, (tile + 1) * TILE)
        x = ref[:, :, low:high]
        if high - low < TILE:
            x = jnp.concatenate([x, jnp.zeros((count, 2, TILE - (high - low)), x.dtype)], axis=2)
        at = tile * 2 * count
        scratch[at : at + 2 * count, :] = x.reshape(2 * count, TILE).astype(F32)
        for k in range(2):
            rows[k].append(scratch[pl.ds(at + k, count, stride=2), :][:, : high - low])
    return [jnp.concatenate(x, axis=1) for x in rows]


def write_pairs(ref, pair, scratch):
    count, _, lanes = ref.shape
    for tile in range(-(-lanes // TILE)):
        low, high = tile * TILE, min(lanes, (tile + 1) * TILE)
        at = tile * 2 * count
        for k in range(2):
            x = pair[k][:, low:high]
            if high - low < TILE:
                x = jnp.concatenate([x, jnp.zeros((count, TILE - (high - low)), F32)], axis=1)
            scratch[pl.ds(at + k, count, stride=2), :] = x
        x = scratch[at : at + 2 * count, :].astype(BF16).reshape(count, 2, TILE)
        ref[:, :, low:high] = x[:, :, : high - low]


def write_plain(ref, pair):
    for k in range(2):
        ref[:, k, :] = pair[k].astype(BF16)


def swap_cells(ref, n):
    return jnp.concatenate([ref[pl.ds(j, n, stride=n), :] for j in range(n)], axis=0)


def project(normed, w_in, proj_ref, sent_ref, order, pairs_out):
    h = sent_ref.shape[0]
    proj = dot(w_in, normed, 0, 0)
    proj_ref[...] = proj
    gated = [jax.nn.sigmoid(proj[at + h : at + 2 * h]) * proj[at : at + h] for at in (0, 2 * h)]
    write_plain(sent_ref, [gated[place] for place in order])


def project_back(x, proj_ref, w_in, gl, gr, grad_gate):
    h = gl.shape[0]
    normed, rstd = norm(x)
    sa = jax.nn.sigmoid(proj_ref[h : 2 * h, :])
    sb = jax.nn.sigmoid(proj_ref[3 * h : 4 * h, :])
    gate = jax.nn.sigmoid(proj_ref[4 * h :, :])
    gla, grb = gl * sa, gr * sb
    grad = jnp.concatenate(
        [
            gla,
            gla * proj_ref[:h, :] * (1 - sa),
            grb,
            grb * proj_ref[2 * h : 3 * h, :] * (1 - sb),
            grad_gate * gate * (1 - gate),
        ],
        axis=0,
    ).astype(BF16)
    return norm_back(dot(w_in, grad, 1, 0), normed, rstd), normed.astype(BF16), grad


def finish(mixed, w_out):
    normed, rstd = norm(mixed)
    post = normed.astype(BF16)
    return dot(w_out, post, 0, 0), normed, rstd, post


def finish_back(grad_new, gate, out, normed, rstd, post, w_out):
    grad_gate = grad_new * out
    grad_proj = (grad_new * gate).astype(BF16)
    grad_w = dot(post, grad_proj, 1, 1)
    return norm_back(dot(w_out, grad_proj, 1, 0), normed, rstd), grad_gate, grad_w


def owners(count, h):
    run = h // SPLIT
    return [(at, (at // run // PARTS) * run, run) for at in range(0, count, run)]


def summed(got_ref):
    count = got_ref.shape[0]
    h = count // PARTS
    def total(k):
        sums = {}
        for at, channel, run in owners(count, h):
            part = got_ref[at : at + run, k, :].astype(F32)
            sums[channel] = sums[channel] + part if channel in sums else part
        return jnp.concatenate(list(sums.values()), axis=0)

    return jnp.concatenate([total(0), total(1)], axis=1)


def to_owners(x):
    h, cells = x.shape
    runs = [x[channel : channel + run] for _, channel, run in owners(PARTS * h, h)]
    x = jnp.concatenate(runs, axis=0)
    return [x[:, : cells // 2], x[:, cells // 2 :]]


def turn_pair(pair_ref, pair_t_ref, normed_ref):
    x = pair_ref[...].T
    pair_t_ref[...] = x
    normed_ref[...] = norm(x)[0].astype(BF16)


def start_one(normed_ref, w_ref, sent_ref, proj_ref, pairs_out):
    project(normed_ref[...], w_ref[...], proj_ref, sent_ref, (0, 1), pairs_out)


def middle(
    got_ref, pair_t_ref, proj1_ref, w_out_ref, w_in_ref,
    sent_ref, proj2_ref, mixed_ref, mid_ref, scratch, pairs_out,
):
    h = sent_ref.shape[0]
    mixed = summed(got_ref)
    mixed_ref[...] = mixed
    out, *_ = finish(mixed, w_out_ref[...])
    mid = pair_t_ref[...] + jax.nn.sigmoid(proj1_ref[4 * h :, :]) * out
    scratch[...] = mid.T
    mid = swap_cells(scratch, int(round(scratch.shape[0] ** 0.5))).T
    mid_ref[...] = mid
    project(norm(mid)[0].astype(BF16), w_in_ref[...], proj2_ref, sent_ref, (1, 0), pairs_out)


def turn(
    got_ref, mid_ref, proj_ref, grad_out_ref, w_out_ref,
    new_ref, sent_ref, grad_gate_ref, grad_w_ref, scratch, pairs_out,
):
    h = got_ref.shape[0] // PARTS
    n = new_ref.shape[0]
    out, normed, rstd, post = finish(summed(got_ref), w_out_ref[...])
    gate = jax.nn.sigmoid(proj_ref[4 * h :, :])
    new = (mid_ref[...] + gate * out).T
    scratch[...] = new
    new_ref[...] = swap_cells(scratch, n).reshape(new_ref.shape)
    grad_new = swap_cells(grad_out_ref, n).T
    grad, grad_gate, grad_w = finish_back(grad_new, gate, out, normed, rstd, post, w_out_ref[...])
    write_plain(sent_ref, to_owners(grad))
    grad_gate_ref[...] = grad_gate
    grad_w_ref[...] = grad_w


def between(
    got_ref, mid_ref, proj2_ref, grad_gate2_ref, w_in_ref, grad_out_ref, mixed_ref, proj1_ref, w_out_ref,
    sent_ref, grad_gate_ref, grad_mid_ref, grad_wout_ref, scratch, pairs_out,
):
    h, _, cells = got_ref.shape
    grad_right, grad_left = (got_ref[:, k, :].astype(F32) for k in range(2))
    back, low, grad_proj = project_back(
        mid_ref[...], proj2_ref, w_in_ref[...], grad_left, grad_right, grad_gate2_ref[...]
    )
    scratch[...] = back.T
    n = int(round(scratch.shape[0] ** 0.5))
    grad_mid = (grad_out_ref[...] + swap_cells(scratch, n)).T
    grad_mid_ref[...] = grad_mid
    w_out = w_out_ref[...]
    out, normed, rstd, post = finish(mixed_ref[...], w_out)
    gate = jax.nn.sigmoid(proj1_ref[4 * h :, :])
    grad, grad_gate, grad_w = finish_back(grad_mid, gate, out, normed, rstd, post, w_out)
    grad_gate_ref[...] = grad_gate
    grad_wout_ref[...] = grad_w
    wide = sent_ref.shape[2] - cells // 2
    pairs = low.shape[0] // 2
    weights = [dot(low, grad_proj[at : at + wide], 1, 1) for at in range(0, grad_proj.shape[0], wide)]
    sent = [
        jnp.concatenate(
            [x, jnp.concatenate([w[k * pairs : (k + 1) * pairs] for w in weights], axis=0)], axis=1
        )
        for k, x in enumerate(to_owners(grad))
    ]
    write_plain(sent_ref, sent)


def last(
    got_ref, pair_t_ref, proj_ref, grad_gate_ref, w_in_ref, grad_mid_ref, wout1_ref, wout2_ref,
    pair_grad_ref, weights_ref,
):
    grad_left, grad_right = (got_ref[:, k, :].astype(F32) for k in range(2))
    back, low, grad_proj = project_back(
        pair_t_ref[...], proj_ref, w_in_ref[...], grad_left, grad_right, grad_gate_ref[...]
    )
    c = low.shape[0]
    rows = [dot(low, grad_proj[at : at + c], 1, 1) for at in range(0, grad_proj.shape[0], c)]
    weights_ref[...] = jnp.concatenate(rows + [wout1_ref[...], wout2_ref[...]], axis=0).astype(BF16)
    pair_grad_ref[...] = (grad_mid_ref[...] + back).T


def blocks(x, outer, inner, size, wide):
    rows = []
    for r in range(inner):
        rows.append(
            jnp.concatenate(
                [x[o * size : (o + 1) * size, r * wide : (r + 1) * wide] for o in range(outer)], axis=1
            )
        )
    return jnp.concatenate(rows, axis=0)


def blocks_low(x, outer, inner, size, wide):
    lanes = 128
    width = -(-wide * (outer + inner) // lanes) * lanes
    lane = lax.broadcasted_iota(jnp.int32, (size, lanes), 1)

    def masks(diagonal):
        low, high = diagonal * wide, (diagonal + 1) * wide
        return [
            (t, (lane >= low - t * lanes) & (lane < high - t * lanes))
            for t in range(low // lanes, (high - 1) // lanes + 1)
        ]

    chosen = [masks(diagonal) for diagonal in range(outer + inner - 1)]
    empty = jnp.zeros((size, width - inner * wide), x.dtype)
    turned = []
    for o in range(outer):
        row = jnp.concatenate([x[o * size : (o + 1) * size], empty], axis=1)
        turned.append(pltpu.roll(row, o * wide, 1) if o else row)
    rows = []
    for r in range(inner):
        merged = [None] * (width // lanes)
        for o in range(outer):
            for t, mask in chosen[r + o]:
                piece = turned[o][:, t * lanes : (t + 1) * lanes]
                merged[t] = piece if merged[t] is None else jnp.where(mask, piece, merged[t])
        zero = jnp.zeros((size, lanes), x.dtype)
        row = jnp.concatenate([zero if m is None else m for m in merged], axis=1)
        row = pltpu.roll(row, width - r * wide, 1) if r else row
        rows.append(row[:, : outer * wide])
    return jnp.concatenate(rows, axis=0)


def reorder(ref, outer, inner):
    return jnp.concatenate([ref[pl.ds(r, outer, stride=inner), :] for r in range(inner)], axis=0)


def multiply(size, wide, got_ref, sent_ref, first_out_ref, second_out_ref, scratch, pairs_in, pairs_out):
    part = got_ref.shape[0] // size
    first, second = read_pairs(got_ref, pairs_in)
    first = blocks_low(first.astype(BF16), part, wide, size, wide).astype(BF16)
    scratch[...] = blocks_low(second.astype(BF16), part, wide, size, wide).astype(F32)
    second = reorder(scratch, wide, size).astype(BF16)
    first_out_ref[...] = first
    second_out_ref[...] = second
    out = blocks_low(dot(first, second, 1, 1).astype(BF16), wide, size, size, wide).astype(F32)
    half = sent_ref.shape[2]
    write_pairs(sent_ref, [out[:, :half], out[:, half:]], pairs_out)


def multiply_back(size, wide, got_ref, first_ref, second_ref, *refs):
    sent_ref, (scratch, pairs_out) = refs[0], refs[-2:]
    part = sent_ref.shape[0] // size
    got = [got_ref[:, k, :].astype(F32) for k in range(2)]
    half = wide * wide // 2
    if len(refs) > 3:
        sums = [jnp.sum(x[:, half:], axis=0, keepdims=True) for x in got]
        empty = jnp.zeros((refs[1].shape[0] - len(sums), sums[0].shape[1]), F32)
        refs[1][...] = jnp.concatenate(sums + [empty], axis=0).astype(BF16)
    got = jnp.concatenate([x[:, :half] for x in got], axis=1)
    grad = blocks_low(got.astype(BF16), size, wide, size, wide)
    sent = [blocks(dot(grad, second_ref[...], 1, 0), wide, part, size, wide)]
    scratch[...] = dot(grad, first_ref[...], 0, 0)
    sent.append(blocks(reorder(scratch, size, wide), wide, part, size, wide))
    write_plain(sent_ref, sent)


def total_of(refs):
    total = refs[0].astype(F32)
    for ref in refs[1:]:
        total += ref.astype(F32)
    return total.astype(BF16)


def sum_near(got_ref, slice_ref, sent_ref):
    rows = got_ref.shape[1]
    total = total_of([got_ref[i] for i in range(got_ref.shape[0])])
    wide = slice_ref.shape[1]
    for i in range(sent_ref.shape[0]):
        sent_ref[i, :rows, :] = total
        sent_ref[i, rows:, :wide] = slice_ref[...]
        sent_ref[i, rows:, wide:] = jnp.zeros((slice_ref.shape[0], sent_ref.shape[2] - wide), BF16)


def sum_far(got_ref, sent_ref):
    count = got_ref.shape[0]
    rows = sent_ref.shape[1] - 2 * count
    total = total_of([got_ref[i, :rows, :] for i in range(count)]).astype(F32)
    slices = [got_ref[i, rows:, :].astype(F32)[:2] for i in range(count)]
    total = jnp.concatenate([total] + slices, axis=0).astype(BF16)
    for i in range(sent_ref.shape[0]):
        sent_ref[i] = total


def unpack(scale, far, wide, got_ref, win1_ref, wout1_ref, win2_ref, wout2_ref, scratch):
    near, rows, c = got_ref.shape
    rows -= 2 * far
    scratch[...] = got_ref[:, rows:, :].reshape(scratch.shape).astype(F32)
    flat = jnp.concatenate([got_ref[i, :rows, :] for i in range(near)], axis=0).astype(F32) * scale
    win_rows = win1_ref.shape[1]
    for at in range(0, win_rows, c):
        win1_ref[:, at : at + c] = flat[at : at + c]
    h = wout1_ref.shape[0]
    wout1_ref[...] = flat[win_rows : win_rows + h]
    wout2_ref[...] = flat[win_rows + h :]
    run = far // (win_rows // wide)
    for k in range(2):
        for r in range(run):
            pieces = [
                scratch[pl.ds((at + r) * 2 + k, near, stride=2 * far), :][:, :wide] for at in range(0, far, run)
            ]
            at = (k * run + r) * near
            win2_ref[at : at + near, :] = jnp.concatenate(pieces, axis=1) * scale


def call(body, outs, *args, scratch=()):
    return pl.pallas_call(
        body,
        out_shape=[jax.ShapeDtypeStruct(s, t) for s, t in outs],
        scratch_shapes=[pltpu.VMEM(shape, F32) for shape in scratch],
        compiler_params=pltpu.CompilerParams(vmem_limit_bytes=16 * 1024 * 1024),
    )(*args)


def exchange(x, axes):
    return lax.all_to_all(x, axes, 0, 0, tiled=True)


def local(pair, grad_out, w_in_out, w_out_out, w_in_in, w_out_in):
    n, _, c = pair.shape
    h = w_out_out.shape[0]
    wide = w_in_out.shape[1]
    size = lax.axis_size(ROW)
    cells = n * n
    part = size // PARTS
    low = (h, cells)
    k_shape = (size * n, part * n)
    pair = pair.reshape(cells, c)
    grad_out = grad_out.reshape(cells, c)

    cell_array = ((c, cells), F32)
    near = ((h, 2, cells), BF16)
    all_devices = ((size * size, 2, cells // 2), BF16)

    def product(sent, group, everyone):
        sent, first, second = call(
            functools.partial(multiply, size, n),
            [all_devices, (k_shape, BF16), (k_shape, BF16)],
            exchange(sent, group), scratch=[k_shape, PAIRS, PAIRS],
        )
        return exchange(sent, everyone), first, second

    def product_back(sent, first, second, group, everyone, *extra):
        sent, *rest = call(
            functools.partial(multiply_back, size, n), [near, *extra],
            exchange(sent, everyone), first, second, scratch=[k_shape, PAIRS],
        )
        return (exchange(sent, group), *rest)

    one = (("col_a", "col_b") + ROW, COL + ROW)
    two = (("row_a", "row_b") + COL, ROW + COL)
    slice_wide = wide * c // (2 * size * size)

    pair_t, normed1 = call(turn_pair, [cell_array, ((c, cells), BF16)], pair)
    sent, proj1 = call(start_one, [near, ((wide, cells), F32)], normed1, w_in_out, scratch=[PAIRS])
    got, first1, second1 = product(sent, *one)
    sent, proj2, mixed1, mid_t = call(
        middle,
        [near, ((wide, cells), F32), (low, F32), cell_array],
        got, pair_t, proj1, w_out_out, w_in_in, scratch=[(cells, c), PAIRS],
    )
    got, first2, second2 = product(sent, *two)
    pair_new, sent, grad_gate2, grad_wout_in = call(
        turn,
        [((n, n, c), F32), all_devices, cell_array, ((h, c), F32)],
        got, mid_t, proj2, grad_out, w_out_in, scratch=[(cells, c), PAIRS],
    )
    got, = product_back(sent, first2, second2, *two)
    sent, grad_gate1, grad_mid, grad_wout_out = call(
        between,
        [((size * size, 2, cells // 2 + slice_wide), BF16), cell_array, cell_array, ((h, c), F32)],
        got, mid_t, proj2, grad_gate2, w_in_in, grad_out, mixed1, proj1, w_out_out, scratch=[(cells, c), PAIRS],
    )
    got, win2_slice = product_back(sent, first1, second1, *one, ((8, slice_wide), BF16))
    near_count, far_count = lax.axis_size(NEAR), lax.axis_size(FAR)
    weight_rows = wide + 2 * h
    pair_grad, weights = call(
        last,
        [((cells, c), F32), ((weight_rows, c), BF16)],
        got, pair_t, proj1, grad_gate1, w_in_out, grad_mid, grad_wout_out, grad_wout_in,
    )

    each = weight_rows // near_count
    got = exchange(weights.reshape(near_count, each, c), NEAR)
    sent, = call(sum_near, [((far_count, each + 8, c), BF16)], got, win2_slice)
    sent, = call(sum_far, [((near_count, each + 2 * far_count, c), BF16)], exchange(sent, FAR))
    outs = call(
        functools.partial(unpack, 1.0 / (n * size), far_count, slice_wide),
        [((c, wide), F32), ((h, c), F32), ((c, wide), F32), ((h, c), F32)],
        exchange(sent, NEAR), scratch=[(near_count * 2 * far_count, c)],
    )
    return (pair_new, pair_grad.reshape(n, n, c), *outs)


def solution(mesh):
    rows, cols = (size // (SPLIT * PARTS) for size in mesh.devices.shape)
    fine = Mesh(mesh.devices.reshape(SPLIT, PARTS, rows, SPLIT, PARTS, cols), ROW + COL)
    cell = P(ROW, COL, None)
    return jax.shard_map(
        local,
        mesh=fine,
        in_specs=(cell, cell, P(), P(), P(), P()),
        out_specs=(cell, cell, P(), P(), P(), P()),
        check_vma=False,
    )
```

```python
import functools

import jax
import jax.numpy as jnp
from jax import lax
from jax.experimental import pallas as pl
from jax.experimental.pallas import tpu as pltpu
from jax.sharding import Mesh
from jax.sharding import PartitionSpec as P

EPS = 1e-05
F32 = jnp.float32
BF16 = jnp.bfloat16
TILE = 128
PAIRS = (1536, TILE)
PARTS = 4
SPLIT = 2
ROW = ("row_a", "row_q", "row_b")
COL = ("col_a", "col_q", "col_b")
NEAR = ROW
FAR = COL


def dot(a, b, ca, cb):
    return lax.dot_general(a, b, (((ca,), (cb,)), ((), ())), preferred_element_type=F32)


def norm(x):
    center = x - jnp.mean(x, axis=0, keepdims=True)
    rstd = lax.rsqrt(jnp.mean(center * center, axis=0, keepdims=True) + EPS)
    return center * rstd, rstd


def norm_back(grad, normed, rstd):
    return rstd * (
        grad
        - jnp.mean(grad, axis=0, keepdims=True)
        - normed * jnp.mean(grad * normed, axis=0, keepdims=True)
    )


def read_pairs(ref, scratch):
    count, _, lanes = ref.shape
    rows = [], []
    for tile in range(-(-lanes // TILE)):
        low, high = tile * TILE, min(lanes, (tile + 1) * TILE)
        x = ref[:, :, low:high]
        if high - low < TILE:
            x = jnp.concatenate([x, jnp.zeros((count, 2, TILE - (high - low)), x.dtype)], axis=2)
        at = tile * 2 * count
        scratch[at : at + 2 * count, :] = x.reshape(2 * count, TILE).astype(F32)
        for k in range(2):
            rows[k].append(scratch[pl.ds(at + k, count, stride=2), :][:, : high - low])
    return [jnp.concatenate(x, axis=1) for x in rows]


def write_pairs(ref, pair, scratch):
    count, _, lanes = ref.shape
    for tile in range(-(-lanes // TILE)):
        low, high = tile * TILE, min(lanes, (tile + 1) * TILE)
        at = tile * 2 * count
        for k in range(2):
            x = pair[k][:, low:high]
            if high - low < TILE:
                x = jnp.concatenate([x, jnp.zeros((count, TILE - (high - low)), F32)], axis=1)
            scratch[pl.ds(at + k, count, stride=2), :] = x
        x = scratch[at : at + 2 * count, :].astype(BF16).reshape(count, 2, TILE)
        ref[:, :, low:high] = x[:, :, : high - low]


def write_plain(ref, pair):
    for k in range(2):
        ref[:, k, :] = pair[k].astype(BF16)


def swap_cells(ref, n):
    return jnp.concatenate([ref[pl.ds(j, n, stride=n), :] for j in range(n)], axis=0)


def project(normed, w_in, proj_ref, sent_ref, order, pairs_out):
    h = sent_ref.shape[0]
    proj = dot(w_in, normed, 0, 0)
    proj_ref[...] = proj
    gated = [jax.nn.sigmoid(proj[at + h : at + 2 * h]) * proj[at : at + h] for at in (0, 2 * h)]
    write_plain(sent_ref, [gated[place] for place in order])


def project_back(x, proj_ref, w_in, gl, gr, grad_gate):
    h = gl.shape[0]
    normed, rstd = norm(x)
    sa = jax.nn.sigmoid(proj_ref[h : 2 * h, :])
    sb = jax.nn.sigmoid(proj_ref[3 * h : 4 * h, :])
    gate = jax.nn.sigmoid(proj_ref[4 * h :, :])
    gla, grb = gl * sa, gr * sb
    grad = jnp.concatenate(
        [
            gla,
            gla * proj_ref[:h, :] * (1 - sa),
            grb,
            grb * proj_ref[2 * h : 3 * h, :] * (1 - sb),
            grad_gate * gate * (1 - gate),
        ],
        axis=0,
    ).astype(BF16)
    return norm_back(dot(w_in, grad, 1, 0), normed, rstd), normed.astype(BF16), grad


def finish(mixed, w_out):
    normed, rstd = norm(mixed)
    post = normed.astype(BF16)
    return dot(w_out, post, 0, 0), normed, rstd, post


def finish_back(grad_new, gate, out, normed, rstd, post, w_out):
    grad_gate = grad_new * out
    grad_proj = (grad_new * gate).astype(BF16)
    grad_w = dot(post, grad_proj, 1, 1)
    return norm_back(dot(w_out, grad_proj, 1, 0), normed, rstd), grad_gate, grad_w


def owners(count, h, outer_first=True):
    run = h // (SPLIT * SPLIT)
    found = []
    for at in range(0, count, run):
        a, b = at // (run * SPLIT * PARTS), at // run % SPLIT
        found.append((at, (a * SPLIT + b if outer_first else b * SPLIT + a) * run, run))
    return found


def summed(got_ref, outer_first=True):
    count = got_ref.shape[0]
    h = count // PARTS
    def total(k):
        sums = {}
        for at, channel, run in owners(count, h, outer_first):
            part = got_ref[at : at + run, k, :].astype(F32)
            sums[channel] = sums[channel] + part if channel in sums else part
        return jnp.concatenate([sums[channel] for channel in sorted(sums)], axis=0)

    return jnp.concatenate([total(0), total(1)], axis=1)


def to_owners(x, outer_first=True):
    h, cells = x.shape
    runs = [x[channel : channel + run] for _, channel, run in owners(PARTS * h, h, outer_first)]
    x = jnp.concatenate(runs, axis=0)
    return [x[:, : cells // 2], x[:, cells // 2 :]]


def turn_pair(pair_ref, pair_t_ref, normed_ref):
    x = pair_ref[...].T
    pair_t_ref[...] = x
    normed_ref[...] = norm(x)[0].astype(BF16)


def start_one(normed_ref, w_ref, sent_ref, proj_ref, pairs_out):
    project(normed_ref[...], w_ref[...], proj_ref, sent_ref, (0, 1), pairs_out)


def middle(
    got_ref, pair_t_ref, proj1_ref, w_out_ref, w_in_ref,
    sent_ref, proj2_ref, mixed_ref, mid_ref, scratch, pairs_out,
):
    h = sent_ref.shape[0]
    mixed = summed(got_ref, False)
    mixed_ref[...] = mixed
    out, *_ = finish(mixed, w_out_ref[...])
    mid = pair_t_ref[...] + jax.nn.sigmoid(proj1_ref[4 * h :, :]) * out
    scratch[...] = mid.T
    mid = swap_cells(scratch, int(round(scratch.shape[0] ** 0.5))).T
    mid_ref[...] = mid
    project(norm(mid)[0].astype(BF16), w_in_ref[...], proj2_ref, sent_ref, (1, 0), pairs_out)


def turn(
    got_ref, mid_ref, proj_ref, grad_out_ref, w_out_ref,
    new_ref, sent_ref, grad_gate_ref, grad_w_ref, scratch, pairs_out,
):
    h = got_ref.shape[0] // PARTS
    n = new_ref.shape[0]
    out, normed, rstd, post = finish(summed(got_ref), w_out_ref[...])
    gate = jax.nn.sigmoid(proj_ref[4 * h :, :])
    new = (mid_ref[...] + gate * out).T
    scratch[...] = new
    new_ref[...] = swap_cells(scratch, n).reshape(new_ref.shape)
    grad_new = swap_cells(grad_out_ref, n).T
    grad, grad_gate, grad_w = finish_back(grad_new, gate, out, normed, rstd, post, w_out_ref[...])
    write_plain(sent_ref, to_owners(grad))
    grad_gate_ref[...] = grad_gate
    grad_w_ref[...] = grad_w


def between(
    got_ref, mid_ref, proj2_ref, grad_gate2_ref, w_in_ref, grad_out_ref, mixed_ref, proj1_ref, w_out_ref,
    sent_ref, grad_gate_ref, grad_mid_ref, grad_wout_ref, scratch, pairs_out,
):
    h, _, cells = got_ref.shape
    grad_right, grad_left = (got_ref[:, k, :].astype(F32) for k in range(2))
    back, low, grad_proj = project_back(
        mid_ref[...], proj2_ref, w_in_ref[...], grad_left, grad_right, grad_gate2_ref[...]
    )
    scratch[...] = back.T
    n = int(round(scratch.shape[0] ** 0.5))
    grad_mid = (grad_out_ref[...] + swap_cells(scratch, n)).T
    grad_mid_ref[...] = grad_mid
    w_out = w_out_ref[...]
    out, normed, rstd, post = finish(mixed_ref[...], w_out)
    gate = jax.nn.sigmoid(proj1_ref[4 * h :, :])
    grad, grad_gate, grad_w = finish_back(grad_mid, gate, out, normed, rstd, post, w_out)
    grad_gate_ref[...] = grad_gate
    grad_wout_ref[...] = grad_w
    wide = sent_ref.shape[2] - cells // 2
    pairs = low.shape[0] // 2
    weights = [dot(low, grad_proj[at : at + wide], 1, 1) for at in range(0, grad_proj.shape[0], wide)]
    sent = [
        jnp.concatenate(
            [x, jnp.concatenate([w[k * pairs : (k + 1) * pairs] for w in weights], axis=0)], axis=1
        )
        for k, x in enumerate(to_owners(grad, False))
    ]
    write_plain(sent_ref, sent)


def last(
    got_ref, pair_t_ref, proj_ref, grad_gate_ref, w_in_ref, grad_mid_ref, wout1_ref, wout2_ref,
    pair_grad_ref, weights_ref,
):
    grad_left, grad_right = (got_ref[:, k, :].astype(F32) for k in range(2))
    back, low, grad_proj = project_back(
        pair_t_ref[...], proj_ref, w_in_ref[...], grad_left, grad_right, grad_gate_ref[...]
    )
    c = low.shape[0]
    rows = [dot(low, grad_proj[at : at + c], 1, 1) for at in range(0, grad_proj.shape[0], c)]
    weights_ref[...] = jnp.concatenate(rows + [wout1_ref[...], wout2_ref[...]], axis=0).astype(BF16)
    pair_grad_ref[...] = (grad_mid_ref[...] + back).T


def blocks(x, outer, inner, size, wide):
    rows = []
    for r in range(inner):
        rows.append(
            jnp.concatenate(
                [x[o * size : (o + 1) * size, r * wide : (r + 1) * wide] for o in range(outer)], axis=1
            )
        )
    return jnp.concatenate(rows, axis=0)


def blocks_low(x, outer, inner, size, wide):
    lanes = 128
    width = -(-wide * (outer + inner) // lanes) * lanes
    lane = lax.broadcasted_iota(jnp.int32, (size, lanes), 1)

    def masks(diagonal):
        low, high = diagonal * wide, (diagonal + 1) * wide
        return [
            (t, (lane >= low - t * lanes) & (lane < high - t * lanes))
            for t in range(low // lanes, (high - 1) // lanes + 1)
        ]

    chosen = [masks(diagonal) for diagonal in range(outer + inner - 1)]
    empty = jnp.zeros((size, width - inner * wide), x.dtype)
    turned = []
    for o in range(outer):
        row = jnp.concatenate([x[o * size : (o + 1) * size], empty], axis=1)
        turned.append(pltpu.roll(row, o * wide, 1) if o else row)
    rows = []
    for r in range(inner):
        merged = [None] * (width // lanes)
        for o in range(outer):
            for t, mask in chosen[r + o]:
                piece = turned[o][:, t * lanes : (t + 1) * lanes]
                merged[t] = piece if merged[t] is None else jnp.where(mask, piece, merged[t])
        zero = jnp.zeros((size, lanes), x.dtype)
        row = jnp.concatenate([zero if m is None else m for m in merged], axis=1)
        row = pltpu.roll(row, width - r * wide, 1) if r else row
        rows.append(row[:, : outer * wide])
    return jnp.concatenate(rows, axis=0)


def reorder(ref, outer, inner):
    return jnp.concatenate([ref[pl.ds(r, outer, stride=inner), :] for r in range(inner)], axis=0)


def multiply(size, wide, got_ref, sent_ref, first_out_ref, second_out_ref, scratch, pairs_in, pairs_out):
    part = got_ref.shape[0] // size
    first, second = read_pairs(got_ref, pairs_in)
    first = blocks_low(first.astype(BF16), part, wide, size, wide).astype(BF16)
    scratch[...] = blocks_low(second.astype(BF16), part, wide, size, wide).astype(F32)
    second = reorder(scratch, wide, size).astype(BF16)
    first_out_ref[...] = first
    second_out_ref[...] = second
    out = blocks_low(dot(first, second, 1, 1).astype(BF16), wide, size, size, wide).astype(F32)
    half = sent_ref.shape[2]
    write_pairs(sent_ref, [out[:, :half], out[:, half:]], pairs_out)


def multiply_back(size, wide, got_ref, first_ref, second_ref, *refs):
    sent_ref, (scratch, pairs_out) = refs[0], refs[-2:]
    part = sent_ref.shape[0] // size
    got = [got_ref[:, k, :].astype(F32) for k in range(2)]
    half = wide * wide // 2
    if len(refs) > 3:
        sums = [jnp.sum(x[:, half:], axis=0, keepdims=True) for x in got]
        empty = jnp.zeros((refs[1].shape[0] - len(sums), sums[0].shape[1]), F32)
        refs[1][...] = jnp.concatenate(sums + [empty], axis=0).astype(BF16)
    got = jnp.concatenate([x[:, :half] for x in got], axis=1)
    grad = blocks_low(got.astype(BF16), size, wide, size, wide)
    sent = [blocks(dot(grad, second_ref[...], 1, 0), wide, part, size, wide)]
    scratch[...] = dot(grad, first_ref[...], 0, 0)
    sent.append(blocks(reorder(scratch, size, wide), wide, part, size, wide))
    write_plain(sent_ref, sent)


def total_of(refs):
    total = refs[0].astype(F32)
    for ref in refs[1:]:
        total += ref.astype(F32)
    return total.astype(BF16)


def sum_near(got_ref, slice_ref, sent_ref):
    rows = got_ref.shape[1]
    total = total_of([got_ref[i] for i in range(got_ref.shape[0])])
    wide = slice_ref.shape[1]
    for i in range(sent_ref.shape[0]):
        sent_ref[i, :rows, :] = total
        sent_ref[i, rows:, :wide] = slice_ref[...]
        sent_ref[i, rows:, wide:] = jnp.zeros((slice_ref.shape[0], sent_ref.shape[2] - wide), BF16)


def sum_far(got_ref, sent_ref):
    count = got_ref.shape[0]
    rows = sent_ref.shape[1] - 2 * count
    total = total_of([got_ref[i, :rows, :] for i in range(count)]).astype(F32)
    slices = [got_ref[i, rows:, :].astype(F32)[:2] for i in range(count)]
    total = jnp.concatenate([total] + slices, axis=0).astype(BF16)
    for i in range(sent_ref.shape[0]):
        sent_ref[i] = total


def unpack(scale, far, wide, got_ref, win1_ref, wout1_ref, win2_ref, wout2_ref, scratch):
    near, rows, c = got_ref.shape
    rows -= 2 * far
    scratch[...] = got_ref[:, rows:, :].reshape(scratch.shape).astype(F32)
    flat = jnp.concatenate([got_ref[i, :rows, :] for i in range(near)], axis=0).astype(F32) * scale
    win_rows = win1_ref.shape[1]
    for at in range(0, win_rows, c):
        win1_ref[:, at : at + c] = flat[at : at + c]
    h = wout1_ref.shape[0]
    wout1_ref[...] = flat[win_rows : win_rows + h]
    wout2_ref[...] = flat[win_rows + h :]
    run = far // (win_rows // wide)
    for k in range(2):
        for r in range(run):
            pieces = [
                scratch[pl.ds((at + r) * 2 + k, near, stride=2 * far), :][:, :wide] for at in range(0, far, run)
            ]
            at = (k * run + r) * near
            win2_ref[at : at + near, :] = jnp.concatenate(pieces, axis=1) * scale


def call(body, outs, *args, scratch=()):
    return pl.pallas_call(
        body,
        out_shape=[jax.ShapeDtypeStruct(s, t) for s, t in outs],
        scratch_shapes=[pltpu.VMEM(shape, F32) for shape in scratch],
        compiler_params=pltpu.CompilerParams(vmem_limit_bytes=16 * 1024 * 1024),
    )(*args)


def exchange(x, axes):
    return lax.all_to_all(x, axes, 0, 0, tiled=True)


def local(pair, grad_out, w_in_out, w_out_out, w_in_in, w_out_in):
    n, _, c = pair.shape
    h = w_out_out.shape[0]
    wide = w_in_out.shape[1]
    size = lax.axis_size(ROW)
    cells = n * n
    part = size // PARTS
    low = (h, cells)
    k_shape = (size * n, part * n)
    pair = pair.reshape(cells, c)
    grad_out = grad_out.reshape(cells, c)

    cell_array = ((c, cells), F32)
    near = ((h, 2, cells), BF16)
    all_devices = ((size * size, 2, cells // 2), BF16)

    def product(sent, group, everyone):
        sent, first, second = call(
            functools.partial(multiply, size, n),
            [all_devices, (k_shape, BF16), (k_shape, BF16)],
            exchange(sent, group), scratch=[k_shape, PAIRS, PAIRS],
        )
        return exchange(sent, everyone), first, second

    def product_back(sent, first, second, group, everyone, *extra):
        sent, *rest = call(
            functools.partial(multiply_back, size, n), [near, *extra],
            exchange(sent, everyone), first, second, scratch=[k_shape, PAIRS],
        )
        return (exchange(sent, group), *rest)

    one = (("col_b", "col_a") + ROW, COL + ROW)
    two = (("row_a", "row_b") + COL, ROW + COL)
    slice_wide = wide * c // (2 * size * size)

    pair_t, normed1 = call(turn_pair, [cell_array, ((c, cells), BF16)], pair)
    sent, proj1 = call(start_one, [near, ((wide, cells), F32)], normed1, w_in_out, scratch=[PAIRS])
    got, first1, second1 = product(sent, *one)
    sent, proj2, mixed1, mid_t = call(
        middle,
        [near, ((wide, cells), F32), (low, F32), cell_array],
        got, pair_t, proj1, w_out_out, w_in_in, scratch=[(cells, c), PAIRS],
    )
    got, first2, second2 = product(sent, *two)
    pair_new, sent, grad_gate2, grad_wout_in = call(
        turn,
        [((n, n, c), F32), all_devices, cell_array, ((h, c), F32)],
        got, mid_t, proj2, grad_out, w_out_in, scratch=[(cells, c), PAIRS],
    )
    got, = product_back(sent, first2, second2, *two)
    sent, grad_gate1, grad_mid, grad_wout_out = call(
        between,
        [((size * size, 2, cells // 2 + slice_wide), BF16), cell_array, cell_array, ((h, c), F32)],
        got, mid_t, proj2, grad_gate2, w_in_in, grad_out, mixed1, proj1, w_out_out, scratch=[(cells, c), PAIRS],
    )
    got, win2_slice = product_back(sent, first1, second1, *one, ((8, slice_wide), BF16))
    near_count, far_count = lax.axis_size(NEAR), lax.axis_size(FAR)
    weight_rows = wide + 2 * h
    pair_grad, weights = call(
        last,
        [((cells, c), F32), ((weight_rows, c), BF16)],
        got, pair_t, proj1, grad_gate1, w_in_out, grad_mid, grad_wout_out, grad_wout_in,
    )

    each = weight_rows // near_count
    got = exchange(weights.reshape(near_count, each, c), NEAR)
    sent, = call(sum_near, [((far_count, each + 8, c), BF16)], got, win2_slice)
    sent, = call(sum_far, [((near_count, each + 2 * far_count, c), BF16)], exchange(sent, FAR))
    outs = call(
        functools.partial(unpack, 1.0 / (n * size), far_count, slice_wide),
        [((c, wide), F32), ((h, c), F32), ((c, wide), F32), ((h, c), F32)],
        exchange(sent, NEAR), scratch=[(near_count * 2 * far_count, c)],
    )
    return (pair_new, pair_grad.reshape(n, n, c), *outs)


def solution(mesh):
    rows, cols = (size // (SPLIT * PARTS) for size in mesh.devices.shape)
    fine = Mesh(mesh.devices.reshape(SPLIT, PARTS, rows, SPLIT, PARTS, cols), ROW + COL)
    cell = P(ROW, COL, None)
    return jax.shard_map(
        local,
        mesh=fine,
        in_specs=(cell, cell, P(), P(), P(), P()),
        out_specs=(cell, cell, P(), P(), P(), P()),
        check_vma=False,
    )
```

```python
import functools

import jax
import jax.numpy as jnp
from jax import lax
from jax.experimental import pallas as pl
from jax.experimental.pallas import tpu as pltpu
from jax.sharding import Mesh
from jax.sharding import PartitionSpec as P

EPS = 1e-05
F32 = jnp.float32
BF16 = jnp.bfloat16
TILE = 128
PAIRS = (1536, TILE)
PARTS = 4
SPLIT = 2
ROW = ("row_a", "row_q", "row_b")
COL = ("col_a", "col_q", "col_b")
NEAR = ROW
FAR = COL


def dot(a, b, ca, cb):
    return lax.dot_general(a, b, (((ca,), (cb,)), ((), ())), preferred_element_type=F32)


def norm(x):
    center = x - jnp.mean(x, axis=0, keepdims=True)
    rstd = lax.rsqrt(jnp.mean(center * center, axis=0, keepdims=True) + EPS)
    return center * rstd, rstd


def norm_back(grad, normed, rstd):
    return rstd * (
        grad
        - jnp.mean(grad, axis=0, keepdims=True)
        - normed * jnp.mean(grad * normed, axis=0, keepdims=True)
    )


def read_pairs(ref, scratch):
    count, _, lanes = ref.shape
    rows = [], []
    for tile in range(-(-lanes // TILE)):
        low, high = tile * TILE, min(lanes, (tile + 1) * TILE)
        x = ref[:, :, low:high]
        if high - low < TILE:
            x = jnp.concatenate([x, jnp.zeros((count, 2, TILE - (high - low)), x.dtype)], axis=2)
        at = tile * 2 * count
        scratch[at : at + 2 * count, :] = x.reshape(2 * count, TILE).astype(F32)
        for k in range(2):
            rows[k].append(scratch[pl.ds(at + k, count, stride=2), :][:, : high - low])
    return [jnp.concatenate(x, axis=1) for x in rows]


def write_pairs(ref, pair, scratch):
    count, _, lanes = ref.shape
    for tile in range(-(-lanes // TILE)):
        low, high = tile * TILE, min(lanes, (tile + 1) * TILE)
        at = tile * 2 * count
        for k in range(2):
            x = pair[k][:, low:high]
            if high - low < TILE:
                x = jnp.concatenate([x, jnp.zeros((count, TILE - (high - low)), F32)], axis=1)
            scratch[pl.ds(at + k, count, stride=2), :] = x
        x = scratch[at : at + 2 * count, :].astype(BF16).reshape(count, 2, TILE)
        ref[:, :, low:high] = x[:, :, : high - low]


def write_plain(ref, pair):
    for k in range(2):
        ref[:, k, :] = pair[k].astype(BF16)


def swap_cells(ref, n):
    return jnp.concatenate([ref[pl.ds(j, n, stride=n), :] for j in range(n)], axis=0)


def project(normed, w_in, proj_ref, sent_ref, order, pairs_out):
    h = sent_ref.shape[0]
    proj = dot(w_in, normed, 0, 0)
    proj_ref[...] = proj
    gated = [jax.nn.sigmoid(proj[at + h : at + 2 * h]) * proj[at : at + h] for at in (0, 2 * h)]
    write_plain(sent_ref, [gated[place] for place in order])


def project_back(x, proj_ref, w_in, gl, gr, grad_gate):
    h = gl.shape[0]
    normed, rstd = norm(x)
    sa = jax.nn.sigmoid(proj_ref[h : 2 * h, :])
    sb = jax.nn.sigmoid(proj_ref[3 * h : 4 * h, :])
    gate = jax.nn.sigmoid(proj_ref[4 * h :, :])
    gla, grb = gl * sa, gr * sb
    grad = jnp.concatenate(
        [
            gla,
            gla * proj_ref[:h, :] * (1 - sa),
            grb,
            grb * proj_ref[2 * h : 3 * h, :] * (1 - sb),
            grad_gate * gate * (1 - gate),
        ],
        axis=0,
    ).astype(BF16)
    return norm_back(dot(w_in, grad, 1, 0), normed, rstd), normed.astype(BF16), grad


def finish(mixed, w_out):
    normed, rstd = norm(mixed)
    post = normed.astype(BF16)
    return dot(w_out, post, 0, 0), normed, rstd, post


def finish_back(grad_new, gate, out, normed, rstd, post, w_out):
    grad_gate = grad_new * out
    grad_proj = (grad_new * gate).astype(BF16)
    grad_w = dot(post, grad_proj, 1, 1)
    return norm_back(dot(w_out, grad_proj, 1, 0), normed, rstd), grad_gate, grad_w


def owners(count, h, outer_first=True):
    run = h // (SPLIT * SPLIT)
    found = []
    for at in range(0, count, run):
        a, b = at // (run * SPLIT * PARTS), at // run % SPLIT
        found.append((at, (a * SPLIT + b if outer_first else b * SPLIT + a) * run, run))
    return found


def summed(got_ref, outer_first=True):
    count = got_ref.shape[0]
    h = count // PARTS
    def total(k):
        sums = {}
        for at, channel, run in owners(count, h, outer_first):
            part = got_ref[at : at + run, k, :].astype(F32)
            sums[channel] = sums[channel] + part if channel in sums else part
        return jnp.concatenate([sums[channel] for channel in sorted(sums)], axis=0)

    return jnp.concatenate([total(0), total(1)], axis=1)


def to_owners(x, outer_first=True):
    h, cells = x.shape
    runs = [x[channel : channel + run] for _, channel, run in owners(PARTS * h, h, outer_first)]
    x = jnp.concatenate(runs, axis=0)
    return [x[:, : cells // 2], x[:, cells // 2 :]]


def turn_pair(pair_ref, pair_t_ref, normed_ref):
    x = pair_ref[...].T
    pair_t_ref[...] = x
    normed_ref[...] = norm(x)[0].astype(BF16)


def start_one(normed_ref, w_ref, sent_ref, proj_ref, pairs_out):
    project(normed_ref[...], w_ref[...], proj_ref, sent_ref, (0, 1), pairs_out)


def middle(
    got_ref, pair_t_ref, proj1_ref, w_out_ref, w_in_ref,
    sent_ref, proj2_ref, mixed_ref, mid_ref, scratch, pairs_out,
):
    h = sent_ref.shape[0]
    mixed = summed(got_ref, False)
    mixed_ref[...] = mixed
    out, *_ = finish(mixed, w_out_ref[...])
    mid = pair_t_ref[...] + jax.nn.sigmoid(proj1_ref[4 * h :, :]) * out
    scratch[...] = mid.T
    mid = swap_cells(scratch, int(round(scratch.shape[0] ** 0.5))).T
    mid_ref[...] = mid
    project(norm(mid)[0].astype(BF16), w_in_ref[...], proj2_ref, sent_ref, (1, 0), pairs_out)


def turn(
    got_ref, mid_ref, proj_ref, grad_out_ref, w_out_ref,
    new_ref, sent_ref, grad_gate_ref, grad_w_ref, scratch, pairs_out,
):
    h = got_ref.shape[0] // PARTS
    n = new_ref.shape[0]
    out, normed, rstd, post = finish(summed(got_ref, False), w_out_ref[...])
    gate = jax.nn.sigmoid(proj_ref[4 * h :, :])
    new = (mid_ref[...] + gate * out).T
    scratch[...] = new
    new_ref[...] = swap_cells(scratch, n).reshape(new_ref.shape)
    grad_new = swap_cells(grad_out_ref, n).T
    grad, grad_gate, grad_w = finish_back(grad_new, gate, out, normed, rstd, post, w_out_ref[...])
    write_plain(sent_ref, to_owners(grad, False))
    grad_gate_ref[...] = grad_gate
    grad_w_ref[...] = grad_w


def between(
    got_ref, mid_ref, proj2_ref, grad_gate2_ref, w_in_ref, grad_out_ref, mixed_ref, proj1_ref, w_out_ref,
    sent_ref, grad_gate_ref, grad_mid_ref, grad_wout_ref, scratch, pairs_out,
):
    h, _, cells = got_ref.shape
    grad_right, grad_left = (got_ref[:, k, :].astype(F32) for k in range(2))
    back, low, grad_proj = project_back(
        mid_ref[...], proj2_ref, w_in_ref[...], grad_left, grad_right, grad_gate2_ref[...]
    )
    scratch[...] = back.T
    n = int(round(scratch.shape[0] ** 0.5))
    grad_mid = (grad_out_ref[...] + swap_cells(scratch, n)).T
    grad_mid_ref[...] = grad_mid
    w_out = w_out_ref[...]
    out, normed, rstd, post = finish(mixed_ref[...], w_out)
    gate = jax.nn.sigmoid(proj1_ref[4 * h :, :])
    grad, grad_gate, grad_w = finish_back(grad_mid, gate, out, normed, rstd, post, w_out)
    grad_gate_ref[...] = grad_gate
    grad_wout_ref[...] = grad_w
    wide = sent_ref.shape[2] - cells // 2
    pairs = low.shape[0] // 2
    weights = [dot(low, grad_proj[at : at + wide], 1, 1) for at in range(0, grad_proj.shape[0], wide)]
    sent = [
        jnp.concatenate(
            [x, jnp.concatenate([w[k * pairs : (k + 1) * pairs] for w in weights], axis=0)], axis=1
        )
        for k, x in enumerate(to_owners(grad, False))
    ]
    write_plain(sent_ref, sent)


def last(
    got_ref, pair_t_ref, proj_ref, grad_gate_ref, w_in_ref, grad_mid_ref, wout1_ref, wout2_ref,
    pair_grad_ref, weights_ref,
):
    grad_left, grad_right = (got_ref[:, k, :].astype(F32) for k in range(2))
    back, low, grad_proj = project_back(
        pair_t_ref[...], proj_ref, w_in_ref[...], grad_left, grad_right, grad_gate_ref[...]
    )
    c = low.shape[0]
    rows = [dot(low, grad_proj[at : at + c], 1, 1) for at in range(0, grad_proj.shape[0], c)]
    weights_ref[...] = jnp.concatenate(rows + [wout1_ref[...], wout2_ref[...]], axis=0).astype(BF16)
    pair_grad_ref[...] = (grad_mid_ref[...] + back).T


def blocks(x, outer, inner, size, wide):
    rows = []
    for r in range(inner):
        rows.append(
            jnp.concatenate(
                [x[o * size : (o + 1) * size, r * wide : (r + 1) * wide] for o in range(outer)], axis=1
            )
        )
    return jnp.concatenate(rows, axis=0)


def blocks_low(x, outer, inner, size, wide):
    lanes = 128
    width = -(-wide * (outer + inner) // lanes) * lanes
    lane = lax.broadcasted_iota(jnp.int32, (size, lanes), 1)

    def masks(diagonal):
        low, high = diagonal * wide, (diagonal + 1) * wide
        return [
            (t, (lane >= low - t * lanes) & (lane < high - t * lanes))
            for t in range(low // lanes, (high - 1) // lanes + 1)
        ]

    chosen = [masks(diagonal) for diagonal in range(outer + inner - 1)]
    empty = jnp.zeros((size, width - inner * wide), x.dtype)
    turned = []
    for o in range(outer):
        row = jnp.concatenate([x[o * size : (o + 1) * size], empty], axis=1)
        turned.append(pltpu.roll(row, o * wide, 1) if o else row)
    rows = []
    for r in range(inner):
        merged = [None] * (width // lanes)
        for o in range(outer):
            for t, mask in chosen[r + o]:
                piece = turned[o][:, t * lanes : (t + 1) * lanes]
                merged[t] = piece if merged[t] is None else jnp.where(mask, piece, merged[t])
        zero = jnp.zeros((size, lanes), x.dtype)
        row = jnp.concatenate([zero if m is None else m for m in merged], axis=1)
        row = pltpu.roll(row, width - r * wide, 1) if r else row
        rows.append(row[:, : outer * wide])
    return jnp.concatenate(rows, axis=0)


def reorder(ref, outer, inner):
    return jnp.concatenate([ref[pl.ds(r, outer, stride=inner), :] for r in range(inner)], axis=0)


def multiply(size, wide, got_ref, sent_ref, first_out_ref, second_out_ref, scratch, pairs_in, pairs_out):
    part = got_ref.shape[0] // size
    first, second = read_pairs(got_ref, pairs_in)
    first = blocks_low(first.astype(BF16), part, wide, size, wide).astype(BF16)
    scratch[...] = blocks_low(second.astype(BF16), part, wide, size, wide).astype(F32)
    second = reorder(scratch, wide, size).astype(BF16)
    first_out_ref[...] = first
    second_out_ref[...] = second
    out = blocks_low(dot(first, second, 1, 1).astype(BF16), wide, size, size, wide).astype(F32)
    half = sent_ref.shape[2]
    write_pairs(sent_ref, [out[:, :half], out[:, half:]], pairs_out)


def multiply_back(size, wide, got_ref, first_ref, second_ref, *refs):
    sent_ref, (scratch, pairs_out) = refs[0], refs[-2:]
    part = sent_ref.shape[0] // size
    got = [got_ref[:, k, :].astype(F32) for k in range(2)]
    half = wide * wide // 2
    if len(refs) > 3:
        sums = [jnp.sum(x[:, half:], axis=0, keepdims=True) for x in got]
        empty = jnp.zeros((refs[1].shape[0] - len(sums), sums[0].shape[1]), F32)
        refs[1][...] = jnp.concatenate(sums + [empty], axis=0).astype(BF16)
    got = jnp.concatenate([x[:, :half] for x in got], axis=1)
    grad = blocks_low(got.astype(BF16), size, wide, size, wide)
    sent = [blocks(dot(grad, second_ref[...], 1, 0), wide, part, size, wide)]
    scratch[...] = dot(grad, first_ref[...], 0, 0)
    sent.append(blocks(reorder(scratch, size, wide), wide, part, size, wide))
    write_plain(sent_ref, sent)


def total_of(refs):
    total = refs[0].astype(F32)
    for ref in refs[1:]:
        total += ref.astype(F32)
    return total.astype(BF16)


def sum_near(got_ref, slice_ref, sent_ref):
    rows = got_ref.shape[1]
    total = total_of([got_ref[i] for i in range(got_ref.shape[0])])
    wide = slice_ref.shape[1]
    for i in range(sent_ref.shape[0]):
        sent_ref[i, :rows, :] = total
        sent_ref[i, rows:, :wide] = slice_ref[...]
        sent_ref[i, rows:, wide:] = jnp.zeros((slice_ref.shape[0], sent_ref.shape[2] - wide), BF16)


def sum_far(got_ref, sent_ref):
    count = got_ref.shape[0]
    rows = sent_ref.shape[1] - 2 * count
    total = total_of([got_ref[i, :rows, :] for i in range(count)]).astype(F32)
    slices = [got_ref[i, rows:, :].astype(F32)[:2] for i in range(count)]
    total = jnp.concatenate([total] + slices, axis=0).astype(BF16)
    for i in range(sent_ref.shape[0]):
        sent_ref[i] = total


def unpack(scale, far, wide, got_ref, win1_ref, wout1_ref, win2_ref, wout2_ref, scratch):
    near, rows, c = got_ref.shape
    rows -= 2 * far
    scratch[...] = got_ref[:, rows:, :].reshape(scratch.shape).astype(F32)
    flat = jnp.concatenate([got_ref[i, :rows, :] for i in range(near)], axis=0).astype(F32) * scale
    win_rows = win1_ref.shape[1]
    for at in range(0, win_rows, c):
        win1_ref[:, at : at + c] = flat[at : at + c]
    h = wout1_ref.shape[0]
    wout1_ref[...] = flat[win_rows : win_rows + h]
    wout2_ref[...] = flat[win_rows + h :]
    run = far // (win_rows // wide)
    for k in range(2):
        for r in range(run):
            pieces = [
                scratch[pl.ds((at + r) * 2 + k, near, stride=2 * far), :][:, :wide] for at in range(0, far, run)
            ]
            at = (k * run + r) * near
            win2_ref[at : at + near, :] = jnp.concatenate(pieces, axis=1) * scale


def call(body, outs, *args, scratch=()):
    return pl.pallas_call(
        body,
        out_shape=[jax.ShapeDtypeStruct(s, t) for s, t in outs],
        scratch_shapes=[pltpu.VMEM(shape, F32) for shape in scratch],
        compiler_params=pltpu.CompilerParams(vmem_limit_bytes=16 * 1024 * 1024),
    )(*args)


def exchange(x, axes):
    return lax.all_to_all(x, axes, 0, 0, tiled=True)


def local(pair, grad_out, w_in_out, w_out_out, w_in_in, w_out_in):
    n, _, c = pair.shape
    h = w_out_out.shape[0]
    wide = w_in_out.shape[1]
    size = lax.axis_size(ROW)
    cells = n * n
    part = size // PARTS
    low = (h, cells)
    k_shape = (size * n, part * n)
    pair = pair.reshape(cells, c)
    grad_out = grad_out.reshape(cells, c)

    cell_array = ((c, cells), F32)
    near = ((h, 2, cells), BF16)
    all_devices = ((size * size, 2, cells // 2), BF16)

    def product(sent, group, everyone):
        sent, first, second = call(
            functools.partial(multiply, size, n),
            [all_devices, (k_shape, BF16), (k_shape, BF16)],
            exchange(sent, group), scratch=[k_shape, PAIRS, PAIRS],
        )
        return exchange(sent, everyone), first, second

    def product_back(sent, first, second, group, everyone, *extra):
        sent, *rest = call(
            functools.partial(multiply_back, size, n), [near, *extra],
            exchange(sent, everyone), first, second, scratch=[k_shape, PAIRS],
        )
        return (exchange(sent, group), *rest)

    one = (("col_b", "col_a") + ROW, COL + ROW)
    two = (("row_b", "row_a") + COL, ROW + COL)
    slice_wide = wide * c // (2 * size * size)

    pair_t, normed1 = call(turn_pair, [cell_array, ((c, cells), BF16)], pair)
    sent, proj1 = call(start_one, [near, ((wide, cells), F32)], normed1, w_in_out, scratch=[PAIRS])
    got, first1, second1 = product(sent, *one)
    sent, proj2, mixed1, mid_t = call(
        middle,
        [near, ((wide, cells), F32), (low, F32), cell_array],
        got, pair_t, proj1, w_out_out, w_in_in, scratch=[(cells, c), PAIRS],
    )
    got, first2, second2 = product(sent, *two)
    pair_new, sent, grad_gate2, grad_wout_in = call(
        turn,
        [((n, n, c), F32), all_devices, cell_array, ((h, c), F32)],
        got, mid_t, proj2, grad_out, w_out_in, scratch=[(cells, c), PAIRS],
    )
    got, = product_back(sent, first2, second2, *two)
    sent, grad_gate1, grad_mid, grad_wout_out = call(
        between,
        [((size * size, 2, cells // 2 + slice_wide), BF16), cell_array, cell_array, ((h, c), F32)],
        got, mid_t, proj2, grad_gate2, w_in_in, grad_out, mixed1, proj1, w_out_out, scratch=[(cells, c), PAIRS],
    )
    got, win2_slice = product_back(sent, first1, second1, *one, ((8, slice_wide), BF16))
    near_count, far_count = lax.axis_size(NEAR), lax.axis_size(FAR)
    weight_rows = wide + 2 * h
    pair_grad, weights = call(
        last,
        [((cells, c), F32), ((weight_rows, c), BF16)],
        got, pair_t, proj1, grad_gate1, w_in_out, grad_mid, grad_wout_out, grad_wout_in,
    )

    each = weight_rows // near_count
    got = exchange(weights.reshape(near_count, each, c), NEAR)
    sent, = call(sum_near, [((far_count, each + 8, c), BF16)], got, win2_slice)
    sent, = call(sum_far, [((near_count, each + 2 * far_count, c), BF16)], exchange(sent, FAR))
    outs = call(
        functools.partial(unpack, 1.0 / (n * size), far_count, slice_wide),
        [((c, wide), F32), ((h, c), F32), ((c, wide), F32), ((h, c), F32)],
        exchange(sent, NEAR), scratch=[(near_count * 2 * far_count, c)],
    )
    return (pair_new, pair_grad.reshape(n, n, c), *outs)


def solution(mesh):
    rows, cols = (size // (SPLIT * PARTS) for size in mesh.devices.shape)
    fine = Mesh(mesh.devices.reshape(SPLIT, PARTS, rows, SPLIT, PARTS, cols), ROW + COL)
    cell = P(ROW, COL, None)
    return jax.shard_map(
        local,
        mesh=fine,
        in_specs=(cell, cell, P(), P(), P(), P()),
        out_specs=(cell, cell, P(), P(), P(), P()),
        check_vma=False,
    )
```
